128 devices in a mesh: sec: 2 (over core), gx: 8 (over x_hi, z), gy: 8 (over x_lo, y).
Axes of the slice: x: 4 (x_hi: 2, x_lo: 2; x = x_hi * 2 + x_lo), y: 4, z: 4, core: 2. Of those that a mesh axis runs over, the one named last changes fastest.
Arguments:
- slide_thickness: float32 [16, 8, 64, 1024], P(('sec', 'gy'), 'gx'), may hold values from 0.2 to 2
- footprint: int32 [16, 8, 64, 1024], P(('sec', 'gy'), 'gx'), may hold values 0 or 1
- slide_momentum: float32 [16, 8, 64, 1024], P(('sec', 'gy'), 'gx'), may hold values from -1.5 to 1.5
- bed_friction: float32 [16, 8, 64, 1024], P(('sec', 'gy'), 'gx'), may hold values from 0.1 to 1
- surface: float32 [8192, 1024], P(('sec', 'gy'), 'gx'), may hold values from -2 to 2
- flux_x: float32 [3, 8192, 1024], P(None, ('sec', 'gy'), 'gx'), may hold values from -2 to 2
- flux_y: float32 [3, 8192, 1024], P(None, ('sec', 'gy'), 'gx'), may hold values from -2 to 2
- bathy_class: int32 [8192, 1024], P(('sec', 'gy'), 'gx'), may hold values from 0 to 7
- depth_table: float32 [8], replicated, may hold values from 2 to 8
Outputs:
- surface_out: float32 [8192, 1024], P(('sec', 'gy'), 'gx')
- pressure_out: float32 [3, 8192, 1024], P(None, ('sec', 'gy'), 'gx')
- bottom_load: float32 [16, 8, 64, 1024], P(('sec', 'gy'), 'gx')
- thickness_out: float32 [1024, 8192], P(('sec', 'gx', 'gy'))
- momentum_out: float32 [1024, 8192], P(('sec', 'gx', 'gy'))
The draws below stay inside these ranges and needn't reach their ends.
All inputs are finite; a program needn't handle non-finite values. No bound on the sum of `footprint` on one device may be relied on, other than what follows from the above.
Results may differ from the reference program's by a relative error of at most 0.0001.
Values sent between devices are 32-bit elements; how exact they have to be, the bound alone decides.
A program may use at most 128 MiB of HBM per device.

```python
import math
import jax
import jax.numpy as jnp
from jax import lax

LEVELS = 4
SWEEPS = 4
LAYERS = 3
NCLASS = 8
NX = 1024
NY = 8192
BANDS = 16
W = 64
N_GX = 8


def with_ends(result, own_key, smallest, top_value):
    longest = result.shape.index(max(result.shape))
    spots = []
    for shift in (0, 1):
        where = [jax.random.randint(jax.random.fold_in(own_key, axis), (), 0, length) for axis, length in enumerate(result.shape)]
        where[longest] = (where[longest] + shift) % result.shape[longest]
        spots.append(tuple(where))
    return result.at[spots[0]].set(smallest).at[spots[1]].set(top_value)


def shard_levels(key, extent, cuts, least, high):
    loudness, own = 1.0, jax.random.fold_in(key, 6)
    for position, parts in cuts:
        draws = jnp.exp(jax.random.uniform(jax.random.fold_in(own, position), (parts,), jnp.float32, least / len(cuts), high / len(cuts)))
        loudness = loudness * jnp.repeat(draws, extent[position] // parts).reshape([-1 if axis == position else 1 for axis in range(len(extent))])
    return loudness


def noise(stream_key, shape, width, bound, cuts=(), held_as=jnp.bfloat16):
    level = shard_levels(stream_key, shape, cuts, -0.22, 0.18) if cuts else 1.0
    result = jax.random.normal(stream_key, shape, jnp.float32) * width * level
    return jnp.minimum(jnp.maximum(result, -bound), bound).astype(held_as)


def setup_inputs(seed: int = 0) -> dict:
    key_of = jax.random.split(jax.random.key(seed), 10)
    slide_thickness = jnp.clip(0.2 + 1.8 * jax.random.uniform(key_of[0], (BANDS, N_GX, W, NX), jnp.float32) ** shard_levels(key_of[0], (BANDS, N_GX, W, NX), ((0, 16), (1, 8)), -0.2, 0.2), 0.2, 2.0)
    footprint = with_ends((jax.random.randint(key_of[1], (BANDS, N_GX, W, NX), 0, 4) < 3).astype(jnp.int32), jax.random.fold_in(key_of[1], 1), 0, 1)
    slide_momentum = noise(key_of[2], (BANDS, N_GX, W, NX), 0.3, 1.5, ((0, 16), (1, 8)), jnp.float32)
    bed_friction = jnp.clip(jnp.exp(math.log(1.0) - 2.3025851 * jax.random.uniform(key_of[3], (BANDS, N_GX, W, NX), jnp.float32) ** shard_levels(key_of[3], (BANDS, N_GX, W, NX), ((0, 16), (1, 8)), -0.2, 0.2)), 0.1, 1.0)
    surface = noise(key_of[4], (NY, NX), 0.3, 2.0, ((0, 16), (1, 8)), jnp.float32)
    flux_x = noise(key_of[5], (LAYERS, NY, NX), 0.3, 2.0, ((1, 16), (2, 8)), jnp.float32)
    flux_y = noise(key_of[6], (LAYERS, NY, NX), 0.3, 2.0, ((1, 16), (2, 8)), jnp.float32)
    bathy_class = with_ends(jax.random.randint(key_of[7], (NY, NX), 0, NCLASS), jax.random.fold_in(key_of[7], 1), 0, NCLASS - 1).astype(jnp.int32)
    depth_table = jnp.clip(jnp.exp(jax.random.uniform(key_of[8], (NCLASS,), jnp.float32, math.log(2.0), math.log(8.0))), 2.0, 8.0)
    return {"slide_thickness": slide_thickness, "footprint": footprint, "slide_momentum": slide_momentum, "bed_friction": bed_friction, "surface": surface, "flux_x": flux_x, "flux_y": flux_y, "bathy_class": bathy_class, "depth_table": depth_table}


SPREAD = 0.25
GRAVITY_PUSH = 0.4
SOURCE = 2.0
SURFACE_STEP = 0.2
COURANT = 0.25
SLOPE_PULL = 0.5
LAYER_SHARE = (0.2, 0.3, 0.5)

def slide_step(thickness, moment, friction):
    speed = moment / (1.0 + jnp.abs(thickness))
    flux_mass = moment
    flux_moment = moment * speed + 0.5 * thickness * thickness

    def beside(field):
        padded = jnp.pad(field, ((0, 0), (1, 1)))
        return (padded[:, :-2], padded[:, 2:])
    thick_lo, thick_hi = beside(thickness)
    moment_lo, moment_hi = beside(moment)
    mass_lo, mass_hi = beside(flux_mass)
    carry_lo, carry_hi = beside(flux_moment)
    new_thickness = 0.5 * (thick_lo + thick_hi) - 0.5 * COURANT * (mass_hi - mass_lo)
    drag = friction * thickness * speed / jnp.sqrt(speed * speed + 1.0)
    new_moment = 0.5 * (moment_lo + moment_hi) - 0.5 * COURANT * (carry_hi - carry_lo) + COURANT * (SLOPE_PULL * thickness - drag)
    return (new_thickness, new_moment)

def diff_east(padded):
    return (padded[..., 1:-1, 2:] - padded[..., 1:-1, :-2]) * 0.5

def diff_north(padded):
    return (padded[..., 2:, 1:-1] - padded[..., :-2, 1:-1]) * 0.5

def neighbours(padded):
    return padded[..., 1:-1, 2:] + padded[..., 1:-1, :-2] + padded[..., 2:, 1:-1] + padded[..., :-2, 1:-1]

def lookup_depth(bathy_class, depth_table):
    water_depth = jnp.zeros(bathy_class.shape, jnp.float32)
    for class_index in range(depth_table.shape[0]):
        water_depth = water_depth + jnp.where(bathy_class == class_index, depth_table[class_index], 0.0)
    return water_depth

def vertical_inverse(water_depth):
    coupling = 9.0 / (water_depth * water_depth)
    horizontal = 4.0 * SPREAD
    diag_top = horizontal + 3.0 * coupling
    diag_mid = horizontal + 2.0 * coupling
    diag_low = horizontal + coupling
    square = coupling * coupling
    determinant = diag_top * (diag_mid * diag_low - square) - square * diag_low
    return jnp.stack([diag_mid * diag_low - square, coupling * diag_low, square, diag_top * diag_low, coupling * diag_top, diag_top * diag_mid - square]) / determinant

def apply_inverse(inverse, vector):
    top = inverse[0] * vector[0] + inverse[1] * vector[1] + inverse[2] * vector[2]
    mid = inverse[1] * vector[0] + inverse[3] * vector[1] + inverse[4] * vector[2]
    low = inverse[2] * vector[0] + inverse[4] * vector[1] + inverse[5] * vector[2]
    return jnp.stack([top, mid, low])

def pad_cells(field):
    widths = [(0, 0)] * (field.ndim - 2) + [(1, 1), (1, 1)]
    return jnp.pad(field, widths)

def reference(slide_thickness, footprint, slide_momentum, bed_friction, surface, flux_x, flux_y, bathy_class, depth_table):
    thickness = (slide_thickness * footprint.astype(jnp.float32)).reshape(NY, NX)
    moment = slide_momentum.reshape(NY, NX)
    friction = bed_friction.reshape(NY, NX)
    inverse = vertical_inverse(lookup_depth(bathy_class, depth_table))
    share = jnp.array(LAYER_SHARE, dtype=jnp.float32)[:, None, None]
    surface_now = surface
    flux_east = flux_x
    flux_north = flux_y
    pressure = jnp.zeros((LAYERS, NY, NX), jnp.float32)
    bottom_sum = jnp.zeros((NY, NX), jnp.float32)
    for level_index in range(LEVELS):
        new_thickness, moment = slide_step(thickness, moment, friction)
        seafloor_rise = new_thickness - thickness
        thickness = new_thickness
        padded = pad_cells(surface_now)
        flux_east = flux_east - GRAVITY_PUSH * diff_east(padded)
        flux_north = flux_north - GRAVITY_PUSH * diff_north(padded)
        source_term = -(diff_east(pad_cells(flux_east)) + diff_north(pad_cells(flux_north))) + SOURCE * share * seafloor_rise
        for sweep in range(SWEEPS):
            pressure = apply_inverse(inverse, source_term + SPREAD * neighbours(pad_cells(pressure)))
        padded_pressure = pad_cells(pressure)
        flux_east = flux_east - SPREAD * diff_east(padded_pressure)
        flux_north = flux_north - SPREAD * diff_north(padded_pressure)
        surface_now = surface_now - SURFACE_STEP * lax.optimization_barrier(jnp.sum(diff_east(pad_cells(flux_east)) + diff_north(pad_cells(flux_north)), axis=0)) + seafloor_rise
        bottom_sum = bottom_sum + pressure[2]
    bottom_load = (bottom_sum / LEVELS).reshape(BANDS, N_GX, W, NX)
    return (surface_now, pressure, bottom_load, thickness.T, moment.T)
```

```python
import functools

import jax
import jax.numpy as jnp
from jax import lax
from jax.experimental import pallas as pl
from jax.experimental.pallas import tpu as pltpu
from jax.sharding import PartitionSpec as P

LEVELS = 4
SWEEPS = 4
SPREAD = 0.25
GRAVITY_PUSH = 0.4
SOURCE = 2.0
SURFACE_STEP = 0.2
COURANT = 0.25
SLOPE_PULL = 0.5
LAYER_SHARE = (0.2, 0.3, 0.5)

LANES = 128
RIM = 32
PAD = 8
TOP = PAD + RIM
CHUNK = 32
WINDOW = (26, 19, 12, 5)
SHIFT = (26, 71, 102, 119)


def lane_of(shape):
    return lax.broadcasted_iota(jnp.int32, shape, len(shape) - 1)


def turn(value, shift):
    shift = shift % LANES
    return value if shift == 0 else pltpu.roll(value, shift, 1)


def east(value):
    return turn(value, -1) - turn(value, 1)


def edges_of(inner, lane):
    return jnp.where(lane < 64, turn(inner, 32), turn(inner, 96))


def slide_step(h, m, f, first, last):
    width = h.shape[1]

    def lo(v):
        return jnp.where(first, 0.0, pltpu.roll(v, 1, 1))

    def hi(v):
        return jnp.where(last, 0.0, pltpu.roll(v, width - 1, 1))

    u = m / (1.0 + jnp.abs(h))
    fm = m * u + 0.5 * h * h
    m_lo, m_hi = lo(m), hi(m)
    new_h = 0.5 * (lo(h) + hi(h)) - 0.5 * COURANT * (m_hi - m_lo)
    drag = f * h * u / jnp.sqrt(u * u + 1.0)
    new_m = (
        0.5 * (m_lo + m_hi)
        - 0.5 * COURANT * (hi(fm) - lo(fm))
        + COURANT * (SLOPE_PULL * h - drag)
    )
    return new_h, new_m


def kernel(
    dims,
    thick_in, foot_in, mom_in, fric_in, surf_in, fx_in, fy_in, bathy_in, table,
    surf_out, press_out, bottom_out, thick_out, mom_out,
    sl, foot, rise_s, pack_s, hm, hmt, rx, hh,
    eta, uu, vv, bathy, dep, pa, pb, ss, coef, mask, qq, rt, rpk, xs, xr, bq,
    load_sem, out_sem, ys_send, ys_recv, rise_send, rise_recv, rl_send, rl_recv,
    x_send, x_recv, hm_send, hm_recv, h2_send, h2_recv, b_send, b_recv, own_sem,
):
    nsec, ngx, ngy, tile_y, strip_w, cells_x, rc = dims
    bands = nsec * ngy
    rows = tile_y + 2 * RIM
    s, g, y = lax.axis_index("sec"), lax.axis_index("gx"), lax.axis_index("gy")
    b = s * ngy + y

    def along_gx(j):
        return (s, lax.rem(g + j + ngx, ngx), y)

    def along_band(j):
        other = lax.rem(b + j + bands, bands)
        return (other // ngy, g, lax.rem(other, ngy))

    def remote(src, dst, send, recv, device):
        return pltpu.make_async_remote_copy(
            src_ref=src, dst_ref=dst, send_sem=send, recv_sem=recv,
            device_id=device, device_id_type=pl.DeviceIdType.MESH,
        )

    own_rows = pl.ds(TOP, tile_y)
    loads = [
        pltpu.make_async_copy(thick_in.at[0, 0], sl.at[0], load_sem.at[0]),
        pltpu.make_async_copy(foot_in.at[0, 0], foot, load_sem.at[1]),
        pltpu.make_async_copy(mom_in.at[0, 0], sl.at[1], load_sem.at[2]),
        pltpu.make_async_copy(fric_in.at[0, 0], sl.at[2], load_sem.at[3]),
        pltpu.make_async_copy(surf_in, eta.at[0, own_rows], load_sem.at[4]),
        pltpu.make_async_copy(fx_in, uu.at[0, :, own_rows], load_sem.at[5]),
        pltpu.make_async_copy(fy_in, vv.at[0, :, own_rows], load_sem.at[6]),
        pltpu.make_async_copy(bathy_in, bathy.at[own_rows], load_sem.at[7]),
    ]
    for copy in loads:
        copy.start()

    barrier = pltpu.get_barrier_semaphore()
    partners = [along_gx(j) for j in range(1, ngx)] + [along_band(j) for j in range(1, bands)]
    for device in partners:
        pl.semaphore_signal(barrier, inc=1, device_id=device, device_id_type=pl.DeviceIdType.MESH)
    pl.semaphore_wait(barrier, len(partners))

    low, high = pl.ds(PAD, RIM), pl.ds(TOP + tile_y, RIM)
    first_rows, last_rows = pl.ds(0, RIM), pl.ds(tile_y - RIM, RIM)
    y_copies = []
    for n, (src, dst) in enumerate(
        (
            (lambda r: surf_in.at[r], lambda r: eta.at[0, r]),
            (lambda r: fx_in.at[:, r], lambda r: uu.at[0, :, r]),
            (lambda r: fy_in.at[:, r], lambda r: vv.at[0, :, r]),
            (lambda r: bathy_in.at[r], lambda r: bathy.at[r]),
        )
    ):
        y_copies.append(
            remote(src(first_rows), dst(high), ys_send.at[0, n], ys_recv.at[0, n], along_band(-1))
        )
        y_copies.append(
            remote(src(last_rows), dst(low), ys_send.at[1, n], ys_recv.at[1, n], along_band(1))
        )
    for copy in y_copies:
        copy.start()

    for copy in loads[:4]:
        copy.wait()

    def slide_rows(i, carry):
        r = pl.ds(pl.multiple_of(i * 8, 8), 8)
        lane = lane_of((8, cells_x))
        first, last = lane == 0, lane == cells_x - 1
        h = sl[0, r] * foot[r].astype(jnp.float32)
        m, f = sl[1, r], sl[2, r]
        for level in range(LEVELS):
            new_h, m = slide_step(h, m, f, first, last)
            rise = new_h - h
            for j in range(ngx):
                rise_s[level, j, r] = rise[:, j * LANES : (j + 1) * LANES]
            h = new_h
        hm[r] = h
        hm[pl.ds(pl.multiple_of(i * 8 + strip_w, 8), 8)] = m
        return carry

    lax.fori_loop(0, strip_w // 8, slide_rows, 0)

    def strip_rows(j):
        return pl.ds(pl.multiple_of(TOP + j * strip_w, 8), strip_w)

    def rise_copies(n, src, dst):
        copies = []
        for j in range(1, ngx):
            device = along_gx(j)
            copies.append(
                remote(
                    src(device[1]), dst(strip_rows(g)),
                    rise_send.at[n, j], rise_recv.at[n, j], device,
                )
            )
        own = pltpu.make_async_copy(src(g), dst(strip_rows(g)), own_sem.at[n])
        return copies + [own]

    rises = [
        rise_copies(n, lambda j, n=n: rise_s.at[n, j], lambda r, n=n: rt.at[0, n, r])
        for n in range(LEVELS)
    ]
    rises.append(rise_copies(LEVELS, lambda j: pack_s.at[j], lambda r: rpk.at[r]))

    def start(copies):
        for copy in copies:
            copy.start()

    def finish_recv(copies):
        for copy in copies[:-1]:
            copy.wait_recv()
        copies[-1].wait()

    start(rises[0])

    def relays(n, ref):
        return [
            remote(
                ref(pl.ds(TOP, RIM)), ref(high), rl_send.at[0, n], rl_recv.at[0, n], along_band(-1)
            ),
            remote(
                ref(pl.ds(TOP + tile_y - RIM, RIM)), ref(low),
                rl_send.at[1, n], rl_recv.at[1, n], along_band(1),
            ),
        ]

    relay = [relays(n, lambda r, n=n: rt.at[0, n, r]) for n in range(LEVELS)]
    relay.append(relays(LEVELS, lambda r: rpk.at[r]))

    def over_rows(fn, lo=PAD, hi=PAD + rows, step=CHUNK):
        def body(i, carry):
            fn(pl.multiple_of(lo + i * step, 8))
            return carry

        lax.fori_loop(0, (hi - lo) // step, body, 0)

    zero = jnp.zeros((RIM, LANES), jnp.float32)

    def clear_outside(refs):
        @pl.when(b == 0)
        def _():
            for ref in refs:
                ref(low)[...] = zero

        @pl.when(b == bands - 1)
        def _():
            for ref in refs:
                ref(high)[...] = zero

    for copy in loads[4:]:
        copy.wait()
    for copy in y_copies:
        copy.wait_recv()
    clear_outside(
        [lambda r: eta.at[0, r]]
        + [lambda r, k=k: uu.at[0, k, r] for k in range(3)]
        + [lambda r, k=k: vv.at[0, k, r] for k in range(3)]
    )

    def prepare(r):
        here = pl.ds(r, CHUNK)
        lane = lane_of((CHUNK, LANES))
        kind = bathy[here]
        depth = jnp.zeros((CHUNK, LANES), jnp.float32)
        for c in range(table.shape[0]):
            depth = jnp.where(kind == c, table[c], depth)
        dep[0, here] = depth
        dep[1, here] = edges_of(depth, lane)
        eta[1, here] = edges_of(eta[0, here], lane)
        for k in range(3):
            uu[1, k, here] = edges_of(uu[0, k, here], lane)
            vv[1, k, here] = edges_of(vv[0, k, here], lane)
        fields = (
            (eta[0, here], uu[0, 0, here], uu[0, 1, here], uu[0, 2, here]),
            (vv[0, 0, here], vv[0, 1, here], vv[0, 2, here], depth),
        )
        for unit, four in enumerate(fields):
            right = turn(four[0], 32)
            left = four[0]
            for q in range(1, 4):
                right = jnp.where(lane >= 32 * q, turn(four[q], 32 * q + 32), right)
                left = jnp.where(lane >= 32 * q, turn(four[q], 32 * q), left)
            xs[0, unit, here] = right
            xs[1, unit, here] = left
        row = r + lax.broadcasted_iota(jnp.int32, (CHUNK, LANES), 0)
        inside = ((row >= TOP) | (b > 0)) & ((row < TOP + tile_y) | (b < bands - 1))
        inside_columns = ((lane >= 32) | (g > 0)) & ((lane < 96) | (g < ngx - 1))
        mask[0, here] = inside.astype(jnp.float32)
        mask[1, here] = (inside & inside_columns).astype(jnp.float32)

    over_rows(prepare)

    every = pl.ds(PAD, rows)
    x_copies = []
    for unit in range(2):
        x_copies.append(
            remote(
                xs.at[0, unit, every], xr.at[0, unit, every],
                x_send.at[0, unit], x_recv.at[0, unit], along_gx(1),
            )
        )
        x_copies.append(
            remote(
                xs.at[1, unit, every], xr.at[1, unit, every],
                x_send.at[1, unit], x_recv.at[1, unit], along_gx(-1),
            )
        )
    start(x_copies)
    start(rises[1])

    def pack_rows(i, carry):
        r = pl.ds(pl.multiple_of(i * 8, 8), 8)
        lane = lane_of((8, LANES))
        for j in range(ngx):
            packed = None
            at = 0
            for level in range(LEVELS):
                ring = jnp.where(
                    lane < 64,
                    rise_s[level, min(j + 1, ngx - 1), r],
                    rise_s[level, max(j - 1, 0), r],
                )
                ring = turn(ring, SHIFT[level])
                packed = ring if packed is None else jnp.where(lane >= at, ring, packed)
                at += 2 * WINDOW[level]
            pack_s[j, r] = packed
        return carry

    lax.fori_loop(0, strip_w // 8, pack_rows, 0)
    start(rises[4])
    start(rises[2])
    start(rises[3])

    block = ngy * rc
    for j in range(cells_x // LANES):
        turned = hm[:, j * LANES : (j + 1) * LANES].T
        for part in range(LANES // min(block, LANES)):
            size = min(block, LANES)
            x0 = j * LANES + part * size
            group = x0 // block
            hmt[group // ngx, group % ngx, pl.ds(x0 % block, size)] = turned[
                part * size : (part + 1) * size
            ]
    hm_copies = []
    for j in range(1, ngx):
        device = along_gx(j)
        hm_copies.append(
            remote(hmt.at[:, device[1]], rx.at[g], hm_send.at[j], hm_recv.at[j], device)
        )
    hm_copies.append(pltpu.make_async_copy(hmt.at[:, g], rx.at[g], own_sem.at[5]))
    start(hm_copies)

    def invert(p):
        def rows_of(r):
            here = pl.ds(r, CHUNK)
            depth = dep[p, here]
            scale = mask[p, here] * SPREAD
            k = 9.0 / (depth * depth)
            i1 = 1.0 / (1.0 + 3.0 * k)
            l1 = k * i1
            i2 = 1.0 / (1.0 + 2.0 * k - k * l1)
            l2 = k * i2
            i3 = 1.0 / (1.0 + k - k * l2)
            coef[p, 0, here] = l1
            coef[p, 1, here] = l2
            coef[p, 2, here] = i1 * scale
            coef[p, 3, here] = i2 * scale
            coef[p, 4, here] = i3 * scale

        over_rows(rows_of)

    def solve(p, here, v):
        l1, l2 = coef[p, 0, here], coef[p, 1, here]
        y2 = v[1] + l1 * v[0]
        y3 = v[2] + l2 * y2
        x3 = y3 * coef[p, 4, here]
        x2 = y2 * coef[p, 3, here] + l2 * x3
        x1 = v[0] * coef[p, 2, here] + l1 * x2
        return x1, x2, x3

    def predict(p):
        def rows_of(r):
            here, up, down = pl.ds(r, CHUNK), pl.ds(r + 1, CHUNK), pl.ds(r - 1, CHUNK)
            push = mask[p, here] * (0.5 * GRAVITY_PUSH)
            ge = push * east(eta[p, here])
            gn = push * (eta[p, up] - eta[p, down])
            for k in range(3):
                uu[p, k, here] = uu[p, k, here] - ge
                vv[p, k, here] = vv[p, k, here] - gn

        over_rows(rows_of)

    def source(p, level):
        def rows_of(r):
            here, up, down = pl.ds(r, CHUNK), pl.ds(r + 1, CHUNK), pl.ds(r - 1, CHUNK)
            rise = rt[p, level, here]
            v = []
            for k in range(3):
                spread = east(uu[p, k, here]) + (vv[p, k, up] - vv[p, k, down])
                v.append((4.0 * SOURCE * LAYER_SHARE[k]) * rise - 2.0 * spread)
                ss[p, k, here] = v[k]
            if level == 0:
                for k, value in enumerate(solve(p, here, v)):
                    pb[p, k, here] = value

        over_rows(rows_of)

    def sweep(p, old, new):
        def rows_of(r):
            here, up, down = pl.ds(r, CHUNK), pl.ds(r + 1, CHUNK), pl.ds(r - 1, CHUNK)
            v = []
            for k in range(3):
                c = old[p, k, here]
                v.append(
                    (ss[p, k, here] + (turn(c, -1) + turn(c, 1)))
                    + (old[p, k, up] + old[p, k, down])
                )
            for k, value in enumerate(solve(p, here, v)):
                new[p, k, here] = value

        over_rows(rows_of)

    def correct(p, level):
        def rows_of(r):
            here, up, down = pl.ds(r, CHUNK), pl.ds(r + 1, CHUNK), pl.ds(r - 1, CHUNK)
            push = mask[p, here] * (0.5 * SPREAD)
            for k in range(3):
                c = pa[p, k, here]
                uu[p, k, here] = uu[p, k, here] - push * east(c)
                vv[p, k, here] = vv[p, k, here] - push * (pa[p, k, up] - pa[p, k, down])
            c = c * (1.0 / LEVELS)
            qq[p, here] = c if level == 0 else qq[p, here] + c

        over_rows(rows_of)

    def raise_surface(p, level):
        def rows_of(r):
            here, up, down = pl.ds(r, CHUNK), pl.ds(r + 1, CHUNK), pl.ds(r - 1, CHUNK)
            push = mask[p, here] * (0.5 * SURFACE_STEP)
            total = uu[p, 0, here] + uu[p, 1, here] + uu[p, 2, here]
            north = (vv[p, 0, up] + vv[p, 1, up] + vv[p, 2, up]) - (
                vv[p, 0, down] + vv[p, 1, down] + vv[p, 2, down]
            )
            eta[p, here] = eta[p, here] - push * (east(total) + north) + rt[p, level, here]

        over_rows(rows_of)

    def sweeps(p, level):
        if level > 0:
            sweep(p, pa, pb)
        sweep(p, pb, pa)
        sweep(p, pa, pb)
        sweep(p, pb, pa)

    def start_relay(n):
        finish_recv(rises[n])
        start(relay[n])

    def end_relay(n):
        for copy in relay[n]:
            copy.wait_recv()
        if n < LEVELS:
            clear_outside([lambda r: rt.at[0, n, r]])

    def level_of(p, level, between=()):
        predict(p)
        if between:
            between[0]()
        source(p, level)
        if len(between) > 1:
            between[1]()
        sweeps(p, level)
        correct(p, level)
        raise_surface(p, level)

    start_relay(0)
    invert(0)
    level_of(0, 0, (lambda: end_relay(0), lambda: start_relay(1)))

    finish_recv(hm_copies)
    lane64 = lane_of((block, LANES)) < 64
    for part in range(nsec):
        for p in range(ngx // 2):
            one, two = rx[2 * p, part], rx[2 * p + 1, part]
            columns = pl.ds(p * LANES, LANES)
            hh[0, part, :, columns] = jnp.where(lane64, one, turn(two, 64))
            hh[1, part, :, columns] = jnp.where(lane64, turn(one, 64), two)
    band_columns = pl.ds(pl.multiple_of(b * tile_y, LANES), tile_y)
    h2_copies = []
    for which, out in enumerate((thick_out, mom_out)):
        for j in range(1, bands):
            device = along_band(j)
            h2_copies.append(
                remote(
                    hh.at[which, device[0], pl.ds(pl.multiple_of(device[2] * rc, 8), rc)],
                    out.at[:, band_columns],
                    h2_send.at[which, j], h2_recv.at[which, j], device,
                )
            )
    for which, out in enumerate((thick_out, mom_out)):
        h2_copies.append(
            pltpu.make_async_copy(
                hh.at[which, s, pl.ds(pl.multiple_of(y * rc, 8), rc)],
                out.at[:, band_columns],
                own_sem.at[6 + which],
            )
        )
    start(h2_copies)

    level_of(0, 1, (lambda: end_relay(1), lambda: None))

    for n in (4, 2, 3):
        start_relay(n)
    for copy in x_copies:
        copy.wait_recv()
    for n in (4, 2, 3):
        end_relay(n)

    def edge_rows(r):
        here = pl.ds(r, CHUNK)
        lane = lane_of((CHUNK, LANES))
        inside = mask[1, here] > 0.0

        def put(left, inner, right, fill=0.0):
            value = jnp.where(lane < 32, left, jnp.where(lane < 96, inner, right))
            return jnp.where(inside, value, fill)

        left, right = xr[0, 0, here], xr[1, 0, here]
        eta[1, here] = put(left, eta[1, here], turn(right, 96))
        for k in range(3):
            q = k + 1
            uu[1, k, here] = put(turn(left, -32 * q), uu[1, k, here], turn(right, 96 - 32 * q))
        left, right = xr[0, 1, here], xr[1, 1, here]
        for k in range(3):
            vv[1, k, here] = put(turn(left, -32 * k), vv[1, k, here], turn(right, 96 - 32 * k))
        dep[1, here] = put(turn(left, -96), dep[1, here], right, 1.0)
        packed = rpk[here]
        for level in range(LEVELS):
            rt[1, level, here] = put(
                turn(packed, 32 - SHIFT[level]),
                edges_of(rt[0, level, here], lane),
                turn(packed, 96 - SHIFT[level]),
            )

    over_rows(edge_rows)
    invert(1)
    level_of(1, 0)
    level_of(1, 1)

    def merged(inner, edge, lane):
        return jnp.where(
            lane < 16, turn(edge, 96), jnp.where(lane >= 112, turn(edge, 32), inner)
        )

    def merge_rows(r):
        here = pl.ds(r, CHUNK)
        lane = lane_of((CHUNK, LANES))
        refs = [lambda p: eta.at[p]]
        for k in range(3):
            refs += [
                lambda p, k=k: uu.at[p, k], lambda p, k=k: vv.at[p, k], lambda p, k=k: pa.at[p, k]
            ]
        for ref in refs:
            inner, edge = ref(0)[here], ref(1)[here]
            ref(0)[here] = merged(inner, edge, lane)
            ref(1)[here] = jnp.where(
                (lane >= 48) & (lane < 80), edges_of(inner, lane), edge
            )

    over_rows(merge_rows)
    for level in range(2, LEVELS):
        for p in range(2):
            level_of(p, level)

    def last_rows_of(r):
        here = pl.ds(r, CHUNK)
        lane = lane_of((CHUNK, LANES))
        bq[pl.ds(pl.multiple_of(r - TOP, 8), CHUNK)] = merged(qq[0, here], qq[1, here], lane)
        eta[0, here] = merged(eta[0, here], eta[1, here], lane)
        for k in range(3):
            pa[0, k, here] = merged(pa[0, k, here], pa[1, k, here], lane)

    over_rows(last_rows_of, TOP, TOP + tile_y)

    b_copies = []
    columns = pl.ds(pl.multiple_of(g * LANES, LANES), LANES)

    def of_strip(j):
        return bq.at[pl.ds(pl.multiple_of(j * strip_w, 8), strip_w)]

    for j in range(1, ngx):
        device = along_gx(j)
        b_copies.append(
            remote(
                of_strip(device[1]), bottom_out.at[0, 0, :, columns],
                b_send.at[j], b_recv.at[j], device,
            )
        )
    b_copies.append(
        pltpu.make_async_copy(of_strip(g), bottom_out.at[0, 0, :, columns], own_sem.at[8])
    )
    start(b_copies)
    outs = [
        pltpu.make_async_copy(eta.at[0, own_rows], surf_out, out_sem.at[0]),
        pltpu.make_async_copy(pa.at[0, :, own_rows], press_out, out_sem.at[1]),
    ]
    start(outs)
    finish_recv(b_copies)
    for copy in h2_copies[:-2]:
        copy.wait_recv()
    for copy in h2_copies[-2:] + outs:
        copy.wait()
    for copies in rises + [hm_copies, b_copies]:
        for copy in copies[:-1]:
            copy.wait_send()
    for copies in relay + [y_copies, x_copies, h2_copies[:-2]]:
        for copy in copies:
            copy.wait_send()


def shards(
    slide_thickness, footprint, slide_momentum, bed_friction, surface, flux_x, flux_y,
    bathy_class, depth_table,
):
    nsec, ngx, ngy = (lax.axis_size(a) for a in ("sec", "gx", "gy"))
    _, _, strip_w, cells_x = slide_thickness.shape
    tile_y, tile_x = surface.shape
    assert tile_x == LANES and strip_w * 2 == LANES and strip_w * ngx == tile_y
    rc = cells_x // (nsec * ngx * ngy)
    bands = nsec * ngy
    array_rows = tile_y + 2 * TOP
    f32 = jnp.float32
    plane = (2, array_rows, LANES)
    three = (2, 3, array_rows, LANES)
    dma = pltpu.SemaphoreType.DMA
    anywhere = pl.BlockSpec(memory_space=pl.ANY)
    return pl.pallas_call(
        functools.partial(kernel, (nsec, ngx, ngy, tile_y, strip_w, cells_x, rc)),
        out_shape=(
            jax.ShapeDtypeStruct(surface.shape, f32),
            jax.ShapeDtypeStruct(flux_x.shape, f32),
            jax.ShapeDtypeStruct(slide_thickness.shape, f32),
            jax.ShapeDtypeStruct((rc, tile_y * bands), f32),
            jax.ShapeDtypeStruct((rc, tile_y * bands), f32),
        ),
        in_specs=[anywhere] * 8 + [pl.BlockSpec(memory_space=pltpu.SMEM)],
        out_specs=(anywhere,) * 5,
        scratch_shapes=[
            pltpu.VMEM((3, strip_w, cells_x), f32),
            pltpu.VMEM((strip_w, cells_x), jnp.int32),
            pltpu.VMEM((LEVELS, ngx, strip_w, LANES), f32),
            pltpu.VMEM((ngx, strip_w, LANES), f32),
            pltpu.VMEM((2 * strip_w, cells_x), f32),
            pltpu.VMEM((nsec, ngx, ngy * rc, LANES), f32),
            pltpu.VMEM((ngx, nsec, ngy * rc, LANES), f32),
            pltpu.VMEM((2, nsec, ngy * rc, tile_y), f32),
            pltpu.VMEM(plane, f32),
            pltpu.VMEM(three, f32),
            pltpu.VMEM(three, f32),
            pltpu.VMEM((array_rows, LANES), jnp.int32),
            pltpu.VMEM(plane, f32),
            pltpu.VMEM(three, f32),
            pltpu.VMEM(three, f32),
            pltpu.VMEM(three, f32),
            pltpu.VMEM((2, 5, array_rows, LANES), f32),
            pltpu.VMEM(plane, f32),
            pltpu.VMEM(plane, f32),
            pltpu.VMEM((2, LEVELS, array_rows, LANES), f32),
            pltpu.VMEM((array_rows, LANES), f32),
            pltpu.VMEM((2, 2, array_rows, LANES), f32),
            pltpu.VMEM((2, 2, array_rows, LANES), f32),
            pltpu.VMEM((tile_y, LANES), f32),
            dma((8,)),
            dma((2,)),
            dma((2, 4)), dma((2, 4)),
            dma((LEVELS + 1, ngx)), dma((LEVELS + 1, ngx)),
            dma((2, LEVELS + 1)), dma((2, LEVELS + 1)),
            dma((2, 2)), dma((2, 2)),
            dma((ngx,)), dma((ngx,)),
            dma((2, bands)), dma((2, bands)),
            dma((ngx,)), dma((ngx,)),
            dma((9,)),
        ],
        compiler_params=pltpu.CompilerParams(
            collective_id=0, has_side_effects=True, vmem_limit_bytes=56 * 2**20
        ),
    )(
        slide_thickness, footprint, slide_momentum, bed_friction, surface, flux_x, flux_y,
        bathy_class, depth_table,
    )


def solution(mesh):
    strips = P(("sec", "gy"), "gx", None, None)
    tiles = P(("sec", "gy"), "gx")
    layers = P(None, ("sec", "gy"), "gx")
    turned = P(("sec", "gx", "gy"), None)
    return jax.shard_map(
        shards,
        mesh=mesh,
        in_specs=(strips,) * 4 + (tiles, layers, layers, tiles, P()),
        out_specs=(tiles, layers, strips, turned, turned),
        check_vma=False,
    )
```

```python
import functools

import jax
import jax.numpy as jnp
from jax import lax
from jax.experimental import pallas as pl
from jax.experimental.pallas import tpu as pltpu
from jax.sharding import PartitionSpec as P

LEVELS = 4
SWEEPS = 4
SPREAD = 0.25
GRAVITY_PUSH = 0.4
SOURCE = 2.0
SURFACE_STEP = 0.2
COURANT = 0.25
SLOPE_PULL = 0.5
LAYER_SHARE = (0.2, 0.3, 0.5)

LANES = 128
JS = 5
RIM = 32
UNROLL = 4
PAD = 8
TOP = PAD + RIM
WINDOW = (26, 19, 12, 5)
SHIFT = (26, 71, 102, 119)


def lane_of(shape):
    return lax.broadcasted_iota(jnp.int32, shape, len(shape) - 1)


def turn(value, shift):
    shift = shift % LANES
    return value if shift == 0 else pltpu.roll(value, shift, 1)


def slide_step(h, m, f, first, last):
    width = h.shape[1]

    def lo(v):
        return jnp.where(first, 0.0, pltpu.roll(v, 1, 1))

    def hi(v):
        return jnp.where(last, 0.0, pltpu.roll(v, width - 1, 1))

    u = m / (1.0 + jnp.abs(h))
    fm = m * u + 0.5 * h * h
    m_lo, m_hi = lo(m), hi(m)
    new_h = 0.5 * (lo(h) + hi(h)) - 0.5 * COURANT * (m_hi - m_lo)
    drag = f * h * u / jnp.sqrt(u * u + 1.0)
    new_m = (
        0.5 * (m_lo + m_hi)
        - 0.5 * COURANT * (hi(fm) - lo(fm))
        + COURANT * (SLOPE_PULL * h - drag)
    )
    return new_h, new_m


def kernel(
    dims,
    thick_in, foot_in, mom_in, fric_in, surf_in, fx_in, fy_in, bathy_in, table,
    surf_out, press_out, bottom_out, thick_out, mom_out,
    sl, foot, rise_s, pack_s, hm, hmt, rx, hh,
    wide, kinds, wide_rise,
    eta, uu, vv, dep, pa, pb, ss, coef, mask, qq, rt, back,
    load_sem, out_sem, ys_send, ys_recv, rise_send, rise_recv, rl_send, rl_recv,
    x_send, x_recv, hm_send, hm_recv, h2_send, h2_recv, b_send, b_recv, own_sem,
):
    nsec, ngx, ngy, tile_y, strip_w, cells_x, rc = dims
    bands = nsec * ngy
    tile_x = LANES
    s, g, y = lax.axis_index("sec"), lax.axis_index("gx"), lax.axis_index("gy")
    b = s * ngy + y

    def along_gx(j):
        return (s, lax.rem(g + j + ngx, ngx), y)

    def along_band(j):
        other = lax.rem(b + j + bands, bands)
        return (other // ngy, g, lax.rem(other, ngy))

    def remote(src, dst, send, recv, device):
        return pltpu.make_async_remote_copy(
            src_ref=src, dst_ref=dst, send_sem=send, recv_sem=recv,
            device_id=device, device_id_type=pl.DeviceIdType.MESH,
        )

    def start(copies):
        for copy in copies:
            copy.start()

    def finish_recv(copies):
        for copy in copies[:-1]:
            copy.wait_recv()
        copies[-1].wait()

    own_rows = pl.ds(RIM, tile_y)
    loads = [
        pltpu.make_async_copy(thick_in.at[0, 0], sl.at[0], load_sem.at[0]),
        pltpu.make_async_copy(foot_in.at[0, 0], foot, load_sem.at[1]),
        pltpu.make_async_copy(mom_in.at[0, 0], sl.at[1], load_sem.at[2]),
        pltpu.make_async_copy(fric_in.at[0, 0], sl.at[2], load_sem.at[3]),
        pltpu.make_async_copy(surf_in, wide.at[0, own_rows], load_sem.at[4]),
        pltpu.make_async_copy(fx_in, wide.at[pl.ds(1, 3), own_rows], load_sem.at[5]),
        pltpu.make_async_copy(fy_in, wide.at[pl.ds(4, 3), own_rows], load_sem.at[6]),
        pltpu.make_async_copy(bathy_in, kinds.at[own_rows], load_sem.at[7]),
    ]
    start(loads)

    barrier = pltpu.get_barrier_semaphore()
    partners = [along_gx(j) for j in range(1, ngx)] + [along_band(j) for j in range(1, bands)]
    for device in partners:
        pl.semaphore_signal(barrier, inc=1, device_id=device, device_id_type=pl.DeviceIdType.MESH)

    for copy in loads[:4]:
        copy.wait()

    def slide_rows(i, carry):
        r = pl.ds(pl.multiple_of(i * 8, 8), 8)
        lane = lane_of((8, cells_x))
        first, last = lane == 0, lane == cells_x - 1
        h = sl[0, r] * foot[r].astype(jnp.float32)
        m, f = sl[1, r], sl[2, r]
        for level in range(LEVELS):
            new_h, m = slide_step(h, m, f, first, last)
            rise = new_h - h
            for j in range(ngx):
                rise_s[level, j, r] = rise[:, j * LANES : (j + 1) * LANES]
            h = new_h
        hm[r] = h
        hm[pl.ds(pl.multiple_of(i * 8 + strip_w, 8), 8)] = m
        return carry

    lax.fori_loop(0, strip_w // 8, slide_rows, 0)

    def pack_rows(i, carry):
        r = pl.ds(pl.multiple_of(i * 16, 16), 16)
        lane = lane_of((16, LANES))
        for j in range(ngx):
            packed = None
            at = 0
            for level in range(LEVELS):
                ring = jnp.where(
                    lane < 64,
                    rise_s[level, min(j + 1, ngx - 1), r],
                    rise_s[level, max(j - 1, 0), r],
                )
                ring = turn(ring, SHIFT[level])
                packed = ring if packed is None else jnp.where(lane >= at, ring, packed)
                at += 2 * WINDOW[level]
            pack_s[j, r] = packed
        return carry

    lax.fori_loop(0, strip_w // 16, pack_rows, 0)

    pl.semaphore_wait(barrier, len(partners))

    low, high = pl.ds(0, RIM), pl.ds(RIM + tile_y, RIM)
    first_rows, last_rows = pl.ds(0, RIM), pl.ds(tile_y - RIM, RIM)
    y_copies = []
    for n, (src, dst) in enumerate(
        (
            (lambda r: surf_in.at[r], lambda r: wide.at[0, r]),
            (lambda r: fx_in.at[:, r], lambda r: wide.at[pl.ds(1, 3), r]),
            (lambda r: fy_in.at[:, r], lambda r: wide.at[pl.ds(4, 3), r]),
            (lambda r: bathy_in.at[r], lambda r: kinds.at[r]),
        )
    ):
        y_copies.append(
            remote(src(first_rows), dst(high), ys_send.at[0, n], ys_recv.at[0, n], along_band(-1))
        )
        y_copies.append(
            remote(src(last_rows), dst(low), ys_send.at[1, n], ys_recv.at[1, n], along_band(1))
        )
    start(y_copies)

    def strip_rows(j):
        return pl.ds(pl.multiple_of(RIM + j * strip_w, 8), strip_w)

    def rise_copies(n, src):
        copies = []
        for j in range(1, ngx):
            device = along_gx(j)
            copies.append(
                remote(
                    src(device[1]), wide_rise.at[n, strip_rows(g)],
                    rise_send.at[n, j], rise_recv.at[n, j], device,
                )
            )
        own = pltpu.make_async_copy(src(g), wide_rise.at[n, strip_rows(g)], own_sem.at[n])
        return copies + [own]

    rises = [rise_copies(n, lambda j, n=n: rise_s.at[n, j]) for n in range(LEVELS)]
    rises.append(rise_copies(LEVELS, lambda j: pack_s.at[j]))
    relay = []
    for n in range(LEVELS + 1):
        ref = wide_rise.at[n]
        relay.append(
            [
                remote(
                    ref.at[pl.ds(RIM, RIM)], ref.at[high],
                    rl_send.at[0, n], rl_recv.at[0, n], along_band(-1),
                ),
                remote(
                    ref.at[pl.ds(tile_y, RIM)], ref.at[low],
                    rl_send.at[1, n], rl_recv.at[1, n], along_band(1),
                ),
            ]
        )
    order = (0, 4, 1, 2, 3)
    for n in order[:2]:
        start(rises[n])

    zero = jnp.zeros((RIM, LANES), jnp.float32)

    def clear_bands(refs):
        @pl.when(b == 0)
        def _():
            for ref in refs:
                ref[low] = zero

        @pl.when(b == bands - 1)
        def _():
            for ref in refs:
                ref[high] = zero

    for copy in loads[4:]:
        copy.wait()
    for copy in y_copies:
        copy.wait_recv()
    clear_bands([wide.at[f] for f in range(7)])

    def look_up(i, carry):
        here = pl.ds(pl.multiple_of(i * 64, 8), 64)
        kind = kinds[here]
        depth = jnp.full((64, LANES), table[0], jnp.float32)
        for c in range(1, table.shape[0]):
            depth = jnp.where(kind == c, table[c], depth)
        wide[7, here] = depth
        return carry

    lax.fori_loop(0, (tile_y + 2 * RIM) // 64, look_up, 0)

    own_x = pl.ds(TOP, tile_x)
    before, after = pl.ds(PAD, RIM), pl.ds(TOP + tile_x, RIM)

    def turned(src, j):
        return src[pl.ds(j, LANES, stride=JS)].T

    def x_exchange(n, ref):
        lead = (slice(None),) * (len(ref.shape) - 2)
        return [
            remote(
                ref.at[lead + (pl.ds(TOP, RIM),)], ref.at[lead + (after,)],
                x_send.at[0, n], x_recv.at[0, n], along_gx(-1),
            ),
            remote(
                ref.at[lead + (pl.ds(TOP + tile_x - RIM, RIM),)], ref.at[lead + (before,)],
                x_send.at[1, n], x_recv.at[1, n], along_gx(1),
            ),
        ]

    x_copies = [x_exchange(n, ref) for n, ref in enumerate((dep, eta, uu, vv))]
    for j in range(JS):
        dep[j, own_x] = turned(wide.at[7], j)
    start(x_copies[0])
    for j in range(JS):
        eta[j, own_x] = turned(wide.at[0], j)
    start(x_copies[1])
    for k in range(3):
        for j in range(JS):
            uu[k, j, own_x] = turned(wide.at[1 + k], j)
    start(x_copies[2])
    for k in range(3):
        for j in range(JS):
            vv[k, j, own_x] = turned(wide.at[4 + k], j)
    start(x_copies[3])
    for n in order[2:]:
        start(rises[n])

    block = ngy * rc
    size = min(block, LANES)
    for j in range(cells_x // LANES):
        value = hm[:, j * LANES : (j + 1) * LANES].T
        for part in range(LANES // size):
            x0 = j * LANES + part * size
            group = x0 // block
            hmt[group // ngx, group % ngx, pl.ds(x0 % block, size)] = value[
                part * size : (part + 1) * size
            ]
    hm_copies = []
    for j in range(1, ngx):
        device = along_gx(j)
        hm_copies.append(
            remote(hmt.at[:, device[1]], rx.at[g], hm_send.at[j], hm_recv.at[j], device)
        )
    hm_copies.append(pltpu.make_async_copy(hmt.at[:, g], rx.at[g], own_sem.at[5]))

    def over_rows(depth, fn):
        lo = (TOP - depth) // 8
        hi = -(-(TOP + tile_x + depth) // 8)
        count = hi - lo
        group = max(u for u in range(1, UNROLL + 1) if count % u == 0)

        def body(i, carry):
            for u in range(group):
                fn(pl.multiple_of((lo + u) * 8 + i * (8 * group), 8))
            return carry

        lax.fori_loop(0, count // group, body, 0)

    def make_mask(r):
        here = pl.ds(r, 8)
        x = r + lax.broadcasted_iota(jnp.int32, (8, LANES), 0)
        columns = ((x >= TOP) | (g > 0)) & ((x < TOP + tile_x) | (g < ngx - 1))
        for j in range(JS):
            at = JS * lane_of((8, LANES)) + j
            band = ((at >= RIM) | (b > 0)) & ((at < RIM + tile_y) | (b < bands - 1))
            mask[j, here] = (columns & band).astype(jnp.float32)

    over_rows(RIM, make_mask)

    def land(n):
        clear_bands([wide_rise.at[n]])
        if n < LEVELS:
            for j in range(JS):
                rt[n, j, own_x] = turned(wide_rise.at[n], j)
            return
        for j in range(JS):
            value = turned(wide_rise.at[n], j)
            for level in range(LEVELS):
                w, at = WINDOW[level], SHIFT[level]
                rt[level, j, pl.ds(TOP - w, w)] = value[at - w : at]
                rt[level, j, pl.ds(TOP + tile_x, w)] = value[at : at + w]

    for i, n in enumerate(order):
        finish_recv(rises[n])
        start(relay[n])
        if i:
            for copy in relay[order[i - 1]]:
                copy.wait_recv()
            land(order[i - 1])
    for copy in relay[order[-1]]:
        copy.wait_recv()
    land(order[-1])

    for pair in x_copies:
        for copy in pair:
            copy.wait()
    start(hm_copies)

    def clear_columns(rows):
        nothing = jnp.zeros((JS, RIM, LANES), jnp.float32)
        eta[:, rows] = nothing
        for k in range(3):
            uu[k, :, rows] = nothing
            vv[k, :, rows] = nothing
        for level in range(LEVELS):
            rt[level, :, rows] = nothing

    @pl.when(g == 0)
    def _():
        clear_columns(before)

    @pl.when(g == ngx - 1)
    def _():
        clear_columns(after)

    def invert(r):
        here = pl.ds(r, 8)
        for j in range(JS):
            depth = dep[j, here]
            scale = mask[j, here] * SPREAD
            k = 9.0 / (depth * depth)
            i1 = 1.0 / (1.0 + 3.0 * k)
            l1 = k * i1
            i2 = 1.0 / (1.0 + 2.0 * k - k * l1)
            l2 = k * i2
            i3 = 1.0 / (1.0 + k - k * l2)
            coef[0, j, here] = l1
            coef[1, j, here] = l2
            coef[2, j, here] = i1 * scale
            coef[3, j, here] = i2 * scale
            coef[4, j, here] = i3 * scale

    over_rows(26, invert)

    def solve(j, here, v):
        l1, l2 = coef[0, j, here], coef[1, j, here]
        y2 = v[1] + l1 * v[0]
        y3 = v[2] + l2 * y2
        x3 = y3 * coef[4, j, here]
        x2 = y2 * coef[3, j, here] + l2 * x3
        x1 = v[0] * coef[2, j, here] + l1 * x2
        return x1, x2, x3

    def ring(ref, here):
        c = [ref[j, here] for j in range(JS)]
        return [turn(c[-1], 1)] + c + [turn(c[0], -1)]

    def predict(depth):
        def rows_of(r):
            here, up, down = pl.ds(r, 8), pl.ds(r + 1, 8), pl.ds(r - 1, 8)
            c = ring(eta, here)
            for j in range(JS):
                push = mask[j, here] * (0.5 * GRAVITY_PUSH)
                ge = push * (eta[j, up] - eta[j, down])
                gn = push * (c[j + 2] - c[j])
                for k in range(3):
                    uu[k, j, here] = uu[k, j, here] - ge
                    vv[k, j, here] = vv[k, j, here] - gn

        over_rows(depth, rows_of)

    def source(depth, level):
        def rows_of(r):
            here, up, down = pl.ds(r, 8), pl.ds(r + 1, 8), pl.ds(r - 1, 8)
            c = [ring(vv.at[k], here) for k in range(3)]
            for j in range(JS):
                rise = rt[level, j, here]
                v = []
                for k in range(3):
                    spread = (uu[k, j, up] - uu[k, j, down]) + (c[k][j + 2] - c[k][j])
                    v.append((4.0 * SOURCE * LAYER_SHARE[k]) * rise - 2.0 * spread)
                    ss[k, j, here] = v[k]
                if level == 0:
                    for k, value in enumerate(solve(j, here, v)):
                        pb[k, j, here] = value

        over_rows(depth, rows_of)

    def sweep(depth, old, new):
        def rows_of(r):
            here, up, down = pl.ds(r, 8), pl.ds(r + 1, 8), pl.ds(r - 1, 8)
            c = [ring(old.at[k], here) for k in range(3)]
            for j in range(JS):
                v = []
                for k in range(3):
                    v.append(
                        (ss[k, j, here] + (c[k][j + 2] + c[k][j]))
                        + (old[k, j, up] + old[k, j, down])
                    )
                for k, value in enumerate(solve(j, here, v)):
                    new[k, j, here] = value

        over_rows(depth, rows_of)

    def correct(depth, level):
        def rows_of(r):
            here, up, down = pl.ds(r, 8), pl.ds(r + 1, 8), pl.ds(r - 1, 8)
            c = [ring(pa.at[k], here) for k in range(3)]
            for j in range(JS):
                push = mask[j, here] * (0.5 * SPREAD)
                for k in range(3):
                    uu[k, j, here] = uu[k, j, here] - push * (pa[k, j, up] - pa[k, j, down])
                    vv[k, j, here] = vv[k, j, here] - push * (c[k][j + 2] - c[k][j])
                low_layer = c[2][j + 1] * (1.0 / LEVELS)
                qq[j, here] = low_layer if level == 0 else qq[j, here] + low_layer

        over_rows(depth, rows_of)

    def raise_surface(depth, level):
        def rows_of(r):
            here, up, down = pl.ds(r, 8), pl.ds(r + 1, 8), pl.ds(r - 1, 8)
            c = [
                vv[0, j, here] + vv[1, j, here] + vv[2, j, here] for j in range(JS)
            ]
            c = [turn(c[-1], 1)] + c + [turn(c[0], -1)]
            for j in range(JS):
                push = mask[j, here] * (0.5 * SURFACE_STEP)
                total = (uu[0, j, up] + uu[1, j, up] + uu[2, j, up]) - (
                    uu[0, j, down] + uu[1, j, down] + uu[2, j, down]
                )
                eta[j, here] = (
                    eta[j, here] - push * (total + (c[j + 2] - c[j])) + rt[level, j, here]
                )

        over_rows(depth, rows_of)

    def step(level):
        rim = 7 * (LEVELS - 1 - level)
        predict(rim + 6)
        source(rim + 5, level)
        if level > 0:
            sweep(rim + 5, pa, pb)
        sweep(rim + 4, pb, pa)
        sweep(rim + 3, pa, pb)
        sweep(rim + 2, pb, pa)
        correct(rim + 1, level)
        raise_surface(rim, level)

    step(0)

    finish_recv(hm_copies)
    lane64 = lane_of((block, LANES)) < 64
    for part in range(nsec):
        for p in range(ngx // 2):
            one, two = rx[2 * p, part], rx[2 * p + 1, part]
            columns = pl.ds(p * LANES, LANES)
            hh[0, part, :, columns] = jnp.where(lane64, one, turn(two, 64))
            hh[1, part, :, columns] = jnp.where(lane64, turn(one, 64), two)
    band_columns = pl.ds(pl.multiple_of(b * tile_y, LANES), tile_y)
    h2_copies = []
    for which, out in enumerate((thick_out, mom_out)):
        for j in range(1, bands):
            device = along_band(j)
            h2_copies.append(
                remote(
                    hh.at[which, device[0], pl.ds(pl.multiple_of(device[2] * rc, 8), rc)],
                    out.at[:, band_columns],
                    h2_send.at[which, j], h2_recv.at[which, j], device,
                )
            )
    for which, out in enumerate((thick_out, mom_out)):
        h2_copies.append(
            pltpu.make_async_copy(
                hh.at[which, s, pl.ds(pl.multiple_of(y * rc, 8), rc)],
                out.at[:, band_columns],
                own_sem.at[6 + which],
            )
        )
    start(h2_copies)

    for level in range(1, LEVELS):
        step(level)

    def turn_back(n, ref):
        for j in range(JS):
            back[n, pl.ds(j, LANES, stride=JS)] = ref[j, own_x].T

    turn_back(4, qq)
    b_copies = []
    columns = pl.ds(pl.multiple_of(g * LANES, LANES), LANES)
    for j in range(1, ngx):
        device = along_gx(j)
        b_copies.append(
            remote(
                back.at[4, strip_rows(device[1])], bottom_out.at[0, 0, :, columns],
                b_send.at[j], b_recv.at[j], device,
            )
        )
    b_copies.append(
        pltpu.make_async_copy(
            back.at[4, strip_rows(g)], bottom_out.at[0, 0, :, columns], own_sem.at[8]
        )
    )
    start(b_copies)
    for k in range(3):
        turn_back(1 + k, pa.at[k])
    turn_back(0, eta)
    outs = [
        pltpu.make_async_copy(back.at[0, own_rows], surf_out, out_sem.at[0]),
        pltpu.make_async_copy(back.at[pl.ds(1, 3), own_rows], press_out, out_sem.at[1]),
    ]
    start(outs)
    finish_recv(b_copies)
    for copy in h2_copies[:-2]:
        copy.wait_recv()
    for copy in h2_copies[-2:] + outs:
        copy.wait()
    for copies in rises + [hm_copies, b_copies]:
        for copy in copies[:-1]:
            copy.wait_send()
    for copies in relay + [y_copies, h2_copies[:-2]]:
        for copy in copies:
            copy.wait_send()


def write_results(*refs):
    count = len(refs) // 2
    sem = refs[-1]
    copies = [
        pltpu.make_async_copy(refs[n], refs[count + n], sem.at[n]) for n in range(count)
    ]
    for copy in copies:
        copy.start()
    for copy in copies:
        copy.wait()


def shards(
    slide_thickness, footprint, slide_momentum, bed_friction, surface, flux_x, flux_y,
    bathy_class, depth_table,
):
    nsec, ngx, ngy = (lax.axis_size(a) for a in ("sec", "gx", "gy"))
    _, _, strip_w, cells_x = slide_thickness.shape
    tile_y, tile_x = surface.shape
    assert tile_x == LANES and strip_w * 2 == LANES and strip_w * ngx == tile_y
    rc = cells_x // (nsec * ngx * ngy)
    bands = nsec * ngy
    x_rows = tile_x + 2 * TOP
    f32 = jnp.float32
    one = (JS, x_rows, LANES)
    three = (3,) + one
    wide_rows = JS * LANES
    results = (
        jax.ShapeDtypeStruct(surface.shape, f32),
        jax.ShapeDtypeStruct(flux_x.shape, f32),
        jax.ShapeDtypeStruct(slide_thickness.shape, f32),
        jax.ShapeDtypeStruct((rc, tile_y * bands), f32),
        jax.ShapeDtypeStruct((rc, tile_y * bands), f32),
    )
    dma = pltpu.SemaphoreType.DMA
    anywhere = pl.BlockSpec(memory_space=pl.ANY)
    made = pl.pallas_call(
        functools.partial(kernel, (nsec, ngx, ngy, tile_y, strip_w, cells_x, rc)),
        out_shape=results,
        in_specs=[anywhere] * 8 + [pl.BlockSpec(memory_space=pltpu.SMEM)],
        out_specs=(anywhere,) * 5,
        scratch_shapes=[
            pltpu.VMEM((3, strip_w, cells_x), f32),
            pltpu.VMEM((strip_w, cells_x), jnp.int32),
            pltpu.VMEM((LEVELS, ngx, strip_w, LANES), f32),
            pltpu.VMEM((ngx, strip_w, LANES), f32),
            pltpu.VMEM((2 * strip_w, cells_x), f32),
            pltpu.VMEM((nsec, ngx, ngy * rc, LANES), f32),
            pltpu.VMEM((ngx, nsec, ngy * rc, LANES), f32),
            pltpu.VMEM((2, nsec, ngy * rc, tile_y), f32),
            pltpu.VMEM((8, wide_rows, LANES), f32),
            pltpu.VMEM((tile_y + 2 * RIM, LANES), jnp.int32),
            pltpu.VMEM((LEVELS + 1, wide_rows, LANES), f32),
            pltpu.VMEM(one, f32),
            pltpu.VMEM(three, f32),
            pltpu.VMEM(three, f32),
            pltpu.VMEM(one, f32),
            pltpu.VMEM(three, f32),
            pltpu.VMEM(three, f32),
            pltpu.VMEM(three, f32),
            pltpu.VMEM((5,) + one, f32),
            pltpu.VMEM(one, f32),
            pltpu.VMEM(one, f32),
            pltpu.VMEM((LEVELS,) + one, f32),
            pltpu.VMEM((5, wide_rows, LANES), f32),
            dma((8,)),
            dma((2,)),
            dma((2, 4)), dma((2, 4)),
            dma((LEVELS + 1, ngx)), dma((LEVELS + 1, ngx)),
            dma((2, LEVELS + 1)), dma((2, LEVELS + 1)),
            dma((2, 4)), dma((2, 4)),
            dma((ngx,)), dma((ngx,)),
            dma((2, bands)), dma((2, bands)),
            dma((ngx,)), dma((ngx,)),
            dma((9,)),
        ],
        compiler_params=pltpu.CompilerParams(
            collective_id=0, has_side_effects=True, vmem_limit_bytes=56 * 2**20
        ),
    )(
        slide_thickness, footprint, slide_momentum, bed_friction, surface, flux_x, flux_y,
        bathy_class, depth_table,
    )
    return pl.pallas_call(
        write_results,
        out_shape=results,
        in_specs=[anywhere] * 5,
        out_specs=(anywhere,) * 5,
        scratch_shapes=[dma((5,))],
    )(*made)


def solution(mesh):
    strips = P(("sec", "gy"), "gx", None, None)
    tiles = P(("sec", "gy"), "gx")
    layers = P(None, ("sec", "gy"), "gx")
    turned = P(("sec", "gx", "gy"), None)
    return jax.shard_map(
        shards,
        mesh=mesh,
        in_specs=(strips,) * 4 + (tiles, layers, layers, tiles, P()),
        out_specs=(tiles, layers, strips, turned, turned),
        check_vma=False,
    )
```

```python
import functools

import jax
import jax.numpy as jnp
from jax import lax
from jax.experimental import pallas as pl
from jax.experimental.pallas import tpu as pltpu
from jax.sharding import PartitionSpec as P

LEVELS = 4
SWEEPS = 4
SPREAD = 0.25
GRAVITY_PUSH = 0.4
SOURCE = 2.0
SURFACE_STEP = 0.2
COURANT = 0.25
SLOPE_PULL = 0.5
LAYER_SHARE = (0.2, 0.3, 0.5)

LANES = 128
JS = 5
RIM = 32
TILE = 32
UNROLL = 1
PAD = 8
TOP = PAD + RIM
WINDOW = (26, 19, 12, 5)
SHIFT = (26, 71, 102, 119)


def lane_of(shape):
    return lax.broadcasted_iota(jnp.int32, shape, len(shape) - 1)


def turn(value, shift):
    shift = shift % LANES
    return value if shift == 0 else pltpu.roll(value, shift, 1)


def slide_step(h, m, f, first, last):
    width = h.shape[1]

    def lo(v):
        return jnp.where(first, 0.0, pltpu.roll(v, 1, 1))

    def hi(v):
        return jnp.where(last, 0.0, pltpu.roll(v, width - 1, 1))

    u = m / (1.0 + jnp.abs(h))
    fm = m * u + 0.5 * h * h
    m_lo, m_hi = lo(m), hi(m)
    new_h = 0.5 * (lo(h) + hi(h)) - 0.5 * COURANT * (m_hi - m_lo)
    drag = f * h * u / jnp.sqrt(u * u + 1.0)
    new_m = (
        0.5 * (m_lo + m_hi)
        - 0.5 * COURANT * (hi(fm) - lo(fm))
        + COURANT * (SLOPE_PULL * h - drag)
    )
    return new_h, new_m


def kernel(
    dims,
    thick_in, foot_in, mom_in, fric_in, surf_in, fx_in, fy_in, bathy_in, table,
    surf_out, press_out, bottom_out, thick_out, mom_out,
    sl, foot, rise_s, pack_s, hm, hmt, rx, hh,
    wide, kinds, wide_rise,
    eta, uu, vv, dep, pa, pb, ss, coef, mask, qq, rt, back,
    load_sem, out_sem, ys_send, ys_recv, rise_send, rise_recv, rl_send, rl_recv,
    x_send, x_recv, hm_send, hm_recv, h2_send, h2_recv, b_send, b_recv, own_sem,
):
    nsec, ngx, ngy, tile_y, strip_w, cells_x, rc = dims
    bands = nsec * ngy
    tile_x = LANES
    s, g, y = lax.axis_index("sec"), lax.axis_index("gx"), lax.axis_index("gy")
    b = s * ngy + y

    def along_gx(j):
        return (s, lax.rem(g + j + ngx, ngx), y)

    def along_band(j):
        other = lax.rem(b + j + bands, bands)
        return (other // ngy, g, lax.rem(other, ngy))

    def remote(src, dst, send, recv, device):
        return pltpu.make_async_remote_copy(
            src_ref=src, dst_ref=dst, send_sem=send, recv_sem=recv,
            device_id=device, device_id_type=pl.DeviceIdType.MESH,
        )

    def start(copies):
        for copy in copies:
            copy.start()

    def finish_recv(copies):
        for copy in copies[:-1]:
            copy.wait_recv()
        copies[-1].wait()

    own_rows = pl.ds(RIM, tile_y)
    loads = [
        pltpu.make_async_copy(thick_in.at[0, 0], sl.at[0], load_sem.at[0]),
        pltpu.make_async_copy(foot_in.at[0, 0], foot, load_sem.at[1]),
        pltpu.make_async_copy(mom_in.at[0, 0], sl.at[1], load_sem.at[2]),
        pltpu.make_async_copy(fric_in.at[0, 0], sl.at[2], load_sem.at[3]),
        pltpu.make_async_copy(surf_in, wide.at[0, own_rows], load_sem.at[4]),
        pltpu.make_async_copy(fx_in, wide.at[pl.ds(1, 3), own_rows], load_sem.at[5]),
        pltpu.make_async_copy(fy_in, wide.at[pl.ds(4, 3), own_rows], load_sem.at[6]),
        pltpu.make_async_copy(bathy_in, kinds.at[own_rows], load_sem.at[7]),
    ]
    start(loads)

    barrier = pltpu.get_barrier_semaphore()
    partners = [along_gx(j) for j in range(1, ngx)] + [along_band(j) for j in range(1, bands)]
    for device in partners:
        pl.semaphore_signal(barrier, inc=1, device_id=device, device_id_type=pl.DeviceIdType.MESH)

    for copy in loads[:4]:
        copy.wait()

    def slide_rows(i, carry):
        r = pl.ds(pl.multiple_of(i * 8, 8), 8)
        lane = lane_of((8, cells_x))
        first, last = lane == 0, lane == cells_x - 1
        h = sl[0, r] * foot[r].astype(jnp.float32)
        m, f = sl[1, r], sl[2, r]
        for level in range(LEVELS):
            new_h, m = slide_step(h, m, f, first, last)
            rise = new_h - h
            for j in range(ngx):
                rise_s[level, j, r] = rise[:, j * LANES : (j + 1) * LANES]
            h = new_h
        hm[r] = h
        hm[pl.ds(pl.multiple_of(i * 8 + strip_w, 8), 8)] = m
        return carry

    lax.fori_loop(0, strip_w // 8, slide_rows, 0)

    def pack_rows(i, carry):
        r = pl.ds(pl.multiple_of(i * 16, 16), 16)
        lane = lane_of((16, LANES))
        for j in range(ngx):
            packed = None
            at = 0
            for level in range(LEVELS):
                ring = jnp.where(
                    lane < 64,
                    rise_s[level, min(j + 1, ngx - 1), r],
                    rise_s[level, max(j - 1, 0), r],
                )
                ring = turn(ring, SHIFT[level])
                packed = ring if packed is None else jnp.where(lane >= at, ring, packed)
                at += 2 * WINDOW[level]
            pack_s[j, r] = packed
        return carry

    lax.fori_loop(0, strip_w // 16, pack_rows, 0)

    pl.semaphore_wait(barrier, len(partners))

    for copy in loads[4:]:
        copy.wait()
    low, high = pl.ds(0, RIM), pl.ds(RIM + tile_y, RIM)
    first_rows, last_rows = pl.ds(RIM, RIM), pl.ds(tile_y, RIM)
    y_copies = []
    for n, of in enumerate((lambda r: wide.at[pl.ds(0, 7), r], lambda r: kinds.at[r])):
        y_copies.append(
            remote(of(first_rows), of(high), ys_send.at[0, n], ys_recv.at[0, n], along_band(-1))
        )
        y_copies.append(
            remote(of(last_rows), of(low), ys_send.at[1, n], ys_recv.at[1, n], along_band(1))
        )
    start(y_copies)

    def strip_rows(j):
        return pl.ds(pl.multiple_of(RIM + j * strip_w, 8), strip_w)

    def rise_copies(n, src):
        copies = []
        for j in range(1, ngx):
            device = along_gx(j)
            copies.append(
                remote(
                    src(device[1]), wide_rise.at[n, strip_rows(g)],
                    rise_send.at[n, j], rise_recv.at[n, j], device,
                )
            )
        own = pltpu.make_async_copy(src(g), wide_rise.at[n, strip_rows(g)], own_sem.at[n])
        return copies + [own]

    rises = [rise_copies(n, lambda j, n=n: rise_s.at[n, j]) for n in range(LEVELS)]
    rises.append(rise_copies(LEVELS, lambda j: pack_s.at[j]))
    relay = []
    for n in range(LEVELS + 1):
        ref = wide_rise.at[n]
        relay.append(
            [
                remote(
                    ref.at[pl.ds(RIM, RIM)], ref.at[high],
                    rl_send.at[0, n], rl_recv.at[0, n], along_band(-1),
                ),
                remote(
                    ref.at[pl.ds(tile_y, RIM)], ref.at[low],
                    rl_send.at[1, n], rl_recv.at[1, n], along_band(1),
                ),
            ]
        )
    order = (0, 4, 1, 2, 3)
    for n in order:
        start(rises[n])

    zero = jnp.zeros((RIM, LANES), jnp.float32)

    def clear_bands(refs):
        @pl.when(b == 0)
        def _():
            for ref in refs:
                ref[low] = zero

        @pl.when(b == bands - 1)
        def _():
            for ref in refs:
                ref[high] = zero

    for copy in y_copies:
        copy.wait_recv()
    clear_bands([wide.at[f] for f in range(7)])

    def look_up(i, carry):
        here = pl.ds(pl.multiple_of(i * 64, 8), 64)
        kind = kinds[here]
        depth = jnp.full((64, LANES), table[0], jnp.float32)
        for c in range(1, table.shape[0]):
            depth = jnp.where(kind == c, table[c], depth)
        wide[7, here] = depth
        return carry

    lax.fori_loop(0, (tile_y + 2 * RIM) // 64, look_up, 0)

    own_x = pl.ds(TOP, tile_x)
    before, after = pl.ds(PAD, RIM), pl.ds(TOP + tile_x, RIM)

    def turned(src, j):
        return src[pl.ds(j, LANES, stride=JS)].T

    def x_exchange(n, ref, depth):
        lead = (slice(None),) * (len(ref.shape) - 2)
        return [
            remote(
                ref.at[lead + (pl.ds(TOP, depth),)], ref.at[lead + (pl.ds(TOP + tile_x, depth),)],
                x_send.at[0, n], x_recv.at[0, n], along_gx(-1),
            ),
            remote(
                ref.at[lead + (pl.ds(TOP + tile_x - depth, depth),)],
                ref.at[lead + (pl.ds(TOP - depth, depth),)],
                x_send.at[1, n], x_recv.at[1, n], along_gx(1),
            ),
        ]

    x_copies = [x_exchange(n, *of) for n, of in enumerate(((dep, 26), (eta, 28), (uu, 27), (vv, 26)))]
    for j in range(JS):
        dep[j, own_x] = turned(wide.at[7], j)
    start(x_copies[0])
    for j in range(JS):
        eta[j, own_x] = turned(wide.at[0], j)
    start(x_copies[1])
    for k in range(3):
        for j in range(JS):
            uu[k, j, own_x] = turned(wide.at[1 + k], j)
    start(x_copies[2])
    for k in range(3):
        for j in range(JS):
            vv[k, j, own_x] = turned(wide.at[4 + k], j)
    start(x_copies[3])

    block = ngy * rc
    size = min(block, LANES)
    for j in range(cells_x // LANES):
        value = hm[:, j * LANES : (j + 1) * LANES].T
        for part in range(LANES // size):
            x0 = j * LANES + part * size
            group = x0 // block
            hmt[group // ngx, group % ngx, pl.ds(x0 % block, size)] = value[
                part * size : (part + 1) * size
            ]
    hm_copies = []
    for j in range(1, ngx):
        device = along_gx(j)
        hm_copies.append(
            remote(hmt.at[:, device[1]], rx.at[g], hm_send.at[j], hm_recv.at[j], device)
        )
    hm_copies.append(pltpu.make_async_copy(hmt.at[:, g], rx.at[g], own_sem.at[5]))

    def over_rows(depth, fn):
        lo = (TOP - depth) // 8 * 8
        count = -(-(TOP + tile_x + depth - lo) // TILE)
        group = max(u for u in range(1, UNROLL + 1) if count % u == 0)

        def body(i, carry):
            fn(pl.multiple_of(lo + i * TILE, 8))
            return carry

        lax.fori_loop(0, count, body, 0, unroll=group)

    def make_mask(r):
        here = pl.ds(r, TILE)
        x = r + lax.broadcasted_iota(jnp.int32, (TILE, LANES), 0)
        columns = ((x >= TOP) | (g > 0)) & ((x < TOP + tile_x) | (g < ngx - 1))
        for j in range(JS):
            at = JS * lane_of((TILE, LANES)) + j
            band = ((at >= RIM) | (b > 0)) & ((at < RIM + tile_y) | (b < bands - 1))
            mask[j, here] = (columns & band).astype(jnp.float32)

    over_rows(RIM, make_mask)

    def land(n):
        clear_bands([wide_rise.at[n]])
        if n < LEVELS:
            for j in range(JS):
                rt[n, j, own_x] = turned(wide_rise.at[n], j)
            return
        for j in range(JS):
            value = turned(wide_rise.at[n], j)
            for level in range(LEVELS):
                w, at = WINDOW[level], SHIFT[level]
                rt[level, j, pl.ds(TOP - w, w)] = value[at - w : at]
                rt[level, j, pl.ds(TOP + tile_x, w)] = value[at : at + w]

    for i, n in enumerate(order):
        finish_recv(rises[n])
        start(relay[n])
        if i:
            for copy in relay[order[i - 1]]:
                copy.wait_recv()
            land(order[i - 1])
    for copy in relay[order[-1]]:
        copy.wait_recv()
    land(order[-1])

    for pair in x_copies:
        for copy in pair:
            copy.wait()
    start(hm_copies)

    def clear_columns(rows):
        nothing = jnp.zeros((JS, RIM, LANES), jnp.float32)
        eta[:, rows] = nothing
        for k in range(3):
            uu[k, :, rows] = nothing
            vv[k, :, rows] = nothing
        for level in range(LEVELS):
            rt[level, :, rows] = nothing

    @pl.when(g == 0)
    def _():
        clear_columns(before)

    @pl.when(g == ngx - 1)
    def _():
        clear_columns(after)

    def invert(r):
        here = pl.ds(r, TILE)
        for j in range(JS):
            depth = dep[j, here]
            scale = mask[j, here] * SPREAD
            k = 9.0 / (depth * depth)
            i1 = 1.0 / (1.0 + 3.0 * k)
            l1 = k * i1
            i2 = 1.0 / (1.0 + 2.0 * k - k * l1)
            l2 = k * i2
            i3 = 1.0 / (1.0 + k - k * l2)
            coef[0, j, here] = l1
            coef[1, j, here] = l2
            coef[2, j, here] = i1 * scale
            coef[3, j, here] = i2 * scale
            coef[4, j, here] = i3 * scale

    over_rows(26, invert)

    def solve(j, here, v):
        l1, l2 = coef[0, j, here], coef[1, j, here]
        y2 = v[1] + l1 * v[0]
        y3 = v[2] + l2 * y2
        x3 = y3 * coef[4, j, here]
        x2 = y2 * coef[3, j, here] + l2 * x3
        x1 = v[0] * coef[2, j, here] + l1 * x2
        return x1, x2, x3

    def ring(ref, here):
        c = [ref[j, here] for j in range(JS)]
        return [turn(c[-1], 1)] + c + [turn(c[0], -1)]

    def predict(depth):
        def rows_of(r):
            here, up, down = pl.ds(r, TILE), pl.ds(r + 1, TILE), pl.ds(r - 1, TILE)
            c = ring(eta, here)
            for j in range(JS):
                push = mask[j, here] * (0.5 * GRAVITY_PUSH)
                ge = push * (eta[j, up] - eta[j, down])
                gn = push * (c[j + 2] - c[j])
                for k in range(3):
                    uu[k, j, here] = uu[k, j, here] - ge
                    vv[k, j, here] = vv[k, j, here] - gn

        over_rows(depth, rows_of)

    def source(depth, level):
        def rows_of(r):
            here, up, down = pl.ds(r, TILE), pl.ds(r + 1, TILE), pl.ds(r - 1, TILE)
            c = [ring(vv.at[k], here) for k in range(3)]
            for j in range(JS):
                rise = rt[level, j, here]
                v = []
                for k in range(3):
                    spread = (uu[k, j, up] - uu[k, j, down]) + (c[k][j + 2] - c[k][j])
                    v.append((4.0 * SOURCE * LAYER_SHARE[k]) * rise - 2.0 * spread)
                    ss[k, j, here] = v[k]
                if level == 0:
                    for k, value in enumerate(solve(j, here, v)):
                        pb[k, j, here] = value

        over_rows(depth, rows_of)

    def sweep(depth, old, new):
        def rows_of(r):
            here, up, down = pl.ds(r, TILE), pl.ds(r + 1, TILE), pl.ds(r - 1, TILE)
            c = [ring(old.at[k], here) for k in range(3)]
            for j in range(JS):
                v = []
                for k in range(3):
                    v.append(
                        (ss[k, j, here] + (c[k][j + 2] + c[k][j]))
                        + (old[k, j, up] + old[k, j, down])
                    )
                for k, value in enumerate(solve(j, here, v)):
                    new[k, j, here] = value

        over_rows(depth, rows_of)

    def correct(depth, level):
        def rows_of(r):
            here, up, down = pl.ds(r, TILE), pl.ds(r + 1, TILE), pl.ds(r - 1, TILE)
            c = [ring(pa.at[k], here) for k in range(3)]
            for j in range(JS):
                push = mask[j, here] * (0.5 * SPREAD)
                for k in range(3):
                    uu[k, j, here] = uu[k, j, here] - push * (pa[k, j, up] - pa[k, j, down])
                    vv[k, j, here] = vv[k, j, here] - push * (c[k][j + 2] - c[k][j])
                if level < LEVELS - 1:
                    low_layer = c[2][j + 1] * (1.0 / LEVELS)
                    qq[j, here] = low_layer if level == 0 else qq[j, here] + low_layer

        over_rows(depth, rows_of)

    def raise_surface(depth, level):
        def rows_of(r):
            here, up, down = pl.ds(r, TILE), pl.ds(r + 1, TILE), pl.ds(r - 1, TILE)
            c = [
                vv[0, j, here] + vv[1, j, here] + vv[2, j, here] for j in range(JS)
            ]
            c = [turn(c[-1], 1)] + c + [turn(c[0], -1)]
            for j in range(JS):
                push = mask[j, here] * (0.5 * SURFACE_STEP)
                total = (uu[0, j, up] + uu[1, j, up] + uu[2, j, up]) - (
                    uu[0, j, down] + uu[1, j, down] + uu[2, j, down]
                )
                eta[j, here] = (
                    eta[j, here] - push * (total + (c[j + 2] - c[j])) + rt[level, j, here]
                )

        over_rows(depth, rows_of)

    def begin(level):
        rim = 7 * (LEVELS - 1 - level)
        predict(rim + 6)
        source(rim + 5, level)
        if level > 0:
            sweep(rim + 5, pa, pb)
        sweep(rim + 4, pb, pa)
        sweep(rim + 3, pa, pb)
        sweep(rim + 2, pb, pa)

    def step(level):
        rim = 7 * (LEVELS - 1 - level)
        begin(level)
        correct(rim + 1, level)
        raise_surface(rim, level)

    step(0)
    step(1)

    finish_recv(hm_copies)
    lane64 = lane_of((block, LANES)) < 64
    for part in range(nsec):
        for p in range(ngx // 2):
            one, two = rx[2 * p, part], rx[2 * p + 1, part]
            columns = pl.ds(p * LANES, LANES)
            hh[0, part, :, columns] = jnp.where(lane64, one, turn(two, 64))
            hh[1, part, :, columns] = jnp.where(lane64, turn(one, 64), two)
    band_columns = pl.ds(pl.multiple_of(b * tile_y, LANES), tile_y)
    h2_copies = []
    for which, out in enumerate((thick_out, mom_out)):
        for j in range(1, bands):
            device = along_band(j)
            h2_copies.append(
                remote(
                    hh.at[which, device[0], pl.ds(pl.multiple_of(device[2] * rc, 8), rc)],
                    out.at[:, band_columns],
                    h2_send.at[which, j], h2_recv.at[which, j], device,
                )
            )
    for which, out in enumerate((thick_out, mom_out)):
        h2_copies.append(
            pltpu.make_async_copy(
                hh.at[which, s, pl.ds(pl.multiple_of(y * rc, 8), rc)],
                out.at[:, band_columns],
                own_sem.at[6 + which],
            )
        )
    start(h2_copies)

    step(2)

    def turn_back(n, ref):
        for j in range(JS):
            back[n, pl.ds(j, LANES, stride=JS)] = ref[j, own_x].T

    begin(LEVELS - 1)
    for j in range(JS):
        back[4, pl.ds(j, LANES, stride=JS)] = (
            qq[j, own_x] + pa[2, j, own_x] * (1.0 / LEVELS)
        ).T
    b_copies = []
    columns = pl.ds(pl.multiple_of(g * LANES, LANES), LANES)
    for j in range(1, ngx):
        device = along_gx(j)
        b_copies.append(
            remote(
                back.at[4, strip_rows(device[1])], bottom_out.at[0, 0, :, columns],
                b_send.at[j], b_recv.at[j], device,
            )
        )
    b_copies.append(
        pltpu.make_async_copy(
            back.at[4, strip_rows(g)], bottom_out.at[0, 0, :, columns], own_sem.at[8]
        )
    )
    start(b_copies)
    correct(1, LEVELS - 1)
    for k in range(3):
        turn_back(1 + k, pa.at[k])
    outs = [
        pltpu.make_async_copy(back.at[pl.ds(1, 3), own_rows], press_out, out_sem.at[1]),
        pltpu.make_async_copy(back.at[0, own_rows], surf_out, out_sem.at[0]),
    ]
    outs[0].start()
    raise_surface(0, LEVELS - 1)
    turn_back(0, eta)
    outs[1].start()
    finish_recv(b_copies)
    for copy in h2_copies[:-2]:
        copy.wait_recv()
    for copy in h2_copies[-2:] + outs:
        copy.wait()
    for copies in rises + [hm_copies, b_copies]:
        for copy in copies[:-1]:
            copy.wait_send()
    for copies in relay + [y_copies, h2_copies[:-2]]:
        for copy in copies:
            copy.wait_send()


def write_results(*refs):
    count = (len(refs) - 2) // 3
    given, results, held = refs[:count], refs[count : 2 * count], refs[2 * count : 3 * count]
    in_sem, out_sem = refs[3 * count :]
    ins = [pltpu.make_async_copy(given[n], held[n], in_sem.at[n]) for n in range(count)]
    outs = [pltpu.make_async_copy(held[n], results[n], out_sem.at[n]) for n in range(count)]
    for copy in ins:
        copy.start()
    for n in range(count):
        ins[n].wait()
        outs[n].start()
    for copy in outs:
        copy.wait()


def shards(
    slide_thickness, footprint, slide_momentum, bed_friction, surface, flux_x, flux_y,
    bathy_class, depth_table,
):
    nsec, ngx, ngy = (lax.axis_size(a) for a in ("sec", "gx", "gy"))
    _, _, strip_w, cells_x = slide_thickness.shape
    tile_y, tile_x = surface.shape
    assert tile_x == LANES and strip_w * 2 == LANES and strip_w * ngx == tile_y
    rc = cells_x // (nsec * ngx * ngy)
    bands = nsec * ngy
    x_rows = tile_x + 2 * TOP + 16
    f32 = jnp.float32
    one = (JS, x_rows, LANES)
    three = (3,) + one
    wide_rows = JS * LANES
    results = (
        jax.ShapeDtypeStruct(surface.shape, f32),
        jax.ShapeDtypeStruct(flux_x.shape, f32),
        jax.ShapeDtypeStruct(slide_thickness.shape, f32),
        jax.ShapeDtypeStruct((rc, tile_y * bands), f32),
        jax.ShapeDtypeStruct((rc, tile_y * bands), f32),
    )
    dma = pltpu.SemaphoreType.DMA
    anywhere = pl.BlockSpec(memory_space=pl.ANY)
    made = pl.pallas_call(
        functools.partial(kernel, (nsec, ngx, ngy, tile_y, strip_w, cells_x, rc)),
        out_shape=results,
        in_specs=[anywhere] * 8 + [pl.BlockSpec(memory_space=pltpu.SMEM)],
        out_specs=(anywhere,) * 5,
        scratch_shapes=[
            pltpu.VMEM((3, strip_w, cells_x), f32),
            pltpu.VMEM((strip_w, cells_x), jnp.int32),
            pltpu.VMEM((LEVELS, ngx, strip_w, LANES), f32),
            pltpu.VMEM((ngx, strip_w, LANES), f32),
            pltpu.VMEM((2 * strip_w, cells_x), f32),
            pltpu.VMEM((nsec, ngx, ngy * rc, LANES), f32),
            pltpu.VMEM((ngx, nsec, ngy * rc, LANES), f32),
            pltpu.VMEM((2, nsec, ngy * rc, tile_y), f32),
            pltpu.VMEM((8, wide_rows, LANES), f32),
            pltpu.VMEM((tile_y + 2 * RIM, LANES), jnp.int32),
            pltpu.VMEM((LEVELS + 1, wide_rows, LANES), f32),
            pltpu.VMEM(one, f32),
            pltpu.VMEM(three, f32),
            pltpu.VMEM(three, f32),
            pltpu.VMEM(one, f32),
            pltpu.VMEM(three, f32),
            pltpu.VMEM(three, f32),
            pltpu.VMEM(three, f32),
            pltpu.VMEM((5,) + one, f32),
            pltpu.VMEM(one, f32),
            pltpu.VMEM(one, f32),
            pltpu.VMEM((LEVELS,) + one, f32),
            pltpu.VMEM((5, wide_rows, LANES), f32),
            dma((8,)),
            dma((2,)),
            dma((2, 4)), dma((2, 4)),
            dma((LEVELS + 1, ngx)), dma((LEVELS + 1, ngx)),
            dma((2, LEVELS + 1)), dma((2, LEVELS + 1)),
            dma((2, 4)), dma((2, 4)),
            dma((ngx,)), dma((ngx,)),
            dma((2, bands)), dma((2, bands)),
            dma((ngx,)), dma((ngx,)),
            dma((9,)),
        ],
        compiler_params=pltpu.CompilerParams(
            collective_id=0, has_side_effects=True, vmem_limit_bytes=56 * 2**20
        ),
    )(
        slide_thickness, footprint, slide_momentum, bed_friction, surface, flux_x, flux_y,
        bathy_class, depth_table,
    )
    return pl.pallas_call(
        write_results,
        out_shape=results,
        in_specs=[anywhere] * 5,
        out_specs=(anywhere,) * 5,
        scratch_shapes=[pltpu.VMEM(r.shape, f32) for r in results] + [dma((5,)), dma((5,))],
    )(*made)


def solution(mesh):
    strips = P(("sec", "gy"), "gx", None, None)
    tiles = P(("sec", "gy"), "gx")
    layers = P(None, ("sec", "gy"), "gx")
    turned = P(("sec", "gx", "gy"), None)
    return jax.shard_map(
        shards,
        mesh=mesh,
        in_specs=(strips,) * 4 + (tiles, layers, layers, tiles, P()),
        out_specs=(tiles, layers, strips, turned, turned),
        check_vma=False,
    )
```

```python
import functools

import jax
import jax.numpy as jnp
from jax import lax
from jax.experimental import pallas as pl
from jax.experimental.pallas import tpu as pltpu
from jax.sharding import PartitionSpec as P

LEVELS = 4
SWEEPS = 4
SPREAD = 0.25
GRAVITY_PUSH = 0.4
SOURCE = 2.0
SURFACE_STEP = 0.2
COURANT = 0.25
SLOPE_PULL = 0.5
LAYER_SHARE = (0.2, 0.3, 0.5)

LANES = 128
JS = 5
RIM = 32
TILE = 32
UNROLL = 1
PAD = 8
TOP = PAD + RIM
WINDOW = (26, 19, 12, 5)
X_AFTER = {0: (0, 1), 2: (2,), 4: (3,)}
SHIFT = (26, 71, 102, 119)


def lane_of(shape):
    return lax.broadcasted_iota(jnp.int32, shape, len(shape) - 1)


def turn(value, shift):
    shift = shift % LANES
    return value if shift == 0 else pltpu.roll(value, shift, 1)


def slide_step(h, m, f, first, last):
    width = h.shape[1]

    def lo(v):
        return jnp.where(first, 0.0, pltpu.roll(v, 1, 1))

    def hi(v):
        return jnp.where(last, 0.0, pltpu.roll(v, width - 1, 1))

    u = m / (1.0 + jnp.abs(h))
    fm = m * u + 0.5 * h * h
    m_lo, m_hi = lo(m), hi(m)
    new_h = 0.5 * (lo(h) + hi(h)) - 0.5 * COURANT * (m_hi - m_lo)
    drag = f * h * u / jnp.sqrt(u * u + 1.0)
    new_m = (
        0.5 * (m_lo + m_hi)
        - 0.5 * COURANT * (hi(fm) - lo(fm))
        + COURANT * (SLOPE_PULL * h - drag)
    )
    return new_h, new_m


def kernel(
    dims,
    thick_in, foot_in, mom_in, fric_in, surf_in, fx_in, fy_in, bathy_in, table,
    surf_out, press_out, bottom_out, thick_out, mom_out,
    sl, foot, rise_s, pack_s, hm, hmt, rx, hh,
    wide, kinds, wide_rise,
    eta, uu, vv, dep, pa, pb, ss, coef, mask, qq, rt, back,
    load_sem, out_sem, ys_send, ys_recv, rise_send, rise_recv, rl_send, rl_recv,
    x_send, x_recv, hm_send, hm_recv, h2_send, h2_recv, b_send, b_recv, own_sem,
):
    nsec, ngx, ngy, tile_y, strip_w, cells_x, rc = dims
    bands = nsec * ngy
    tile_x = LANES
    s, g, y = lax.axis_index("sec"), lax.axis_index("gx"), lax.axis_index("gy")
    b = s * ngy + y

    def along_gx(j):
        return (s, lax.rem(g + j + ngx, ngx), y)

    def along_band(j):
        other = lax.rem(b + j + bands, bands)
        return (other // ngy, g, lax.rem(other, ngy))

    def remote(src, dst, send, recv, device):
        return pltpu.make_async_remote_copy(
            src_ref=src, dst_ref=dst, send_sem=send, recv_sem=recv,
            device_id=device, device_id_type=pl.DeviceIdType.MESH,
        )

    def start(copies):
        for copy in copies:
            copy.start()

    def to_neighbours(at, count, pairs, what):
        @pl.when(at > 0)
        def _():
            for pair in pairs:
                if what == "recv":
                    pair[1].wait_recv()
                else:
                    pair[0].start() if what == "start" else pair[0].wait_send()

        @pl.when(at < count - 1)
        def _():
            for pair in pairs:
                if what == "recv":
                    pair[0].wait_recv()
                else:
                    pair[1].start() if what == "start" else pair[1].wait_send()

    def finish_recv(copies):
        for copy in copies[:-1]:
            copy.wait_recv()
        copies[-1].wait()

    own_rows = pl.ds(RIM, tile_y)
    loads = [
        pltpu.make_async_copy(thick_in.at[0, 0], sl.at[0], load_sem.at[0]),
        pltpu.make_async_copy(foot_in.at[0, 0], foot, load_sem.at[1]),
        pltpu.make_async_copy(mom_in.at[0, 0], sl.at[1], load_sem.at[2]),
        pltpu.make_async_copy(fric_in.at[0, 0], sl.at[2], load_sem.at[3]),
        pltpu.make_async_copy(surf_in, wide.at[0, own_rows], load_sem.at[4]),
        pltpu.make_async_copy(fx_in, wide.at[pl.ds(1, 3), own_rows], load_sem.at[5]),
        pltpu.make_async_copy(fy_in, wide.at[pl.ds(4, 3), own_rows], load_sem.at[6]),
        pltpu.make_async_copy(bathy_in, kinds.at[own_rows], load_sem.at[7]),
    ]
    start(loads)

    barrier = pltpu.get_barrier_semaphore()
    partners = [along_gx(j) for j in range(1, ngx)] + [along_band(j) for j in range(1, bands)]
    for device in partners:
        pl.semaphore_signal(barrier, inc=1, device_id=device, device_id_type=pl.DeviceIdType.MESH)

    for copy in loads[:4]:
        copy.wait()

    def slide_rows(i, carry):
        r = pl.ds(pl.multiple_of(i * 8, 8), 8)
        lane = lane_of((8, cells_x))
        first, last = lane == 0, lane == cells_x - 1
        h = sl[0, r] * foot[r].astype(jnp.float32)
        m, f = sl[1, r], sl[2, r]
        for level in range(LEVELS):
            new_h, m = slide_step(h, m, f, first, last)
            rise = new_h - h
            for j in range(ngx):
                rise_s[level, j, r] = rise[:, j * LANES : (j + 1) * LANES]
            h = new_h
        hm[r] = h
        hm[pl.ds(pl.multiple_of(i * 8 + strip_w, 8), 8)] = m
        return carry

    lax.fori_loop(0, strip_w // 8, slide_rows, 0)

    pl.semaphore_wait(barrier, len(partners))

    for copy in loads[4:]:
        copy.wait()
    low, high = pl.ds(0, RIM), pl.ds(RIM + tile_y, RIM)
    first_rows, last_rows = pl.ds(RIM, RIM), pl.ds(tile_y, RIM)
    y_copies = []
    for n, of in enumerate((lambda r: wide.at[pl.ds(0, 7), r], lambda r: kinds.at[r])):
        y_copies.append(
            (
                remote(of(first_rows), of(high), ys_send.at[0, n], ys_recv.at[0, n], along_band(-1)),
                remote(of(last_rows), of(low), ys_send.at[1, n], ys_recv.at[1, n], along_band(1)),
            )
        )
    to_neighbours(b, bands, y_copies, "start")

    def strip_rows(j):
        return pl.ds(pl.multiple_of(RIM + j * strip_w, 8), strip_w)

    def rise_copies(n, src):
        copies = []
        for j in range(1, ngx):
            device = along_gx(j)
            copies.append(
                remote(
                    src(device[1]), wide_rise.at[n, strip_rows(g)],
                    rise_send.at[n, j], rise_recv.at[n, j], device,
                )
            )
        own = pltpu.make_async_copy(src(g), wide_rise.at[n, strip_rows(g)], own_sem.at[n])
        return copies + [own]

    rises = [rise_copies(n, lambda j, n=n: rise_s.at[n, j]) for n in range(LEVELS)]
    rises.append(rise_copies(LEVELS, lambda j: pack_s.at[j]))
    relay = []
    for n in range(LEVELS + 1):
        ref = wide_rise.at[n]
        relay.append(
            [
                remote(
                    ref.at[pl.ds(RIM, RIM)], ref.at[high],
                    rl_send.at[0, n], rl_recv.at[0, n], along_band(-1),
                ),
                remote(
                    ref.at[pl.ds(tile_y, RIM)], ref.at[low],
                    rl_send.at[1, n], rl_recv.at[1, n], along_band(1),
                ),
            ]
        )
    order = (0, 1, 4, 2, 3)
    start(rises[0])
    start(rises[1])

    def pack_rows(i, carry):
        r = pl.ds(pl.multiple_of(i * 16, 16), 16)
        lane = lane_of((16, LANES))
        for j in range(ngx):
            packed = None
            at = 0
            for level in range(LEVELS):
                ring = jnp.where(
                    lane < 64,
                    rise_s[level, min(j + 1, ngx - 1), r],
                    rise_s[level, max(j - 1, 0), r],
                )
                ring = turn(ring, SHIFT[level])
                packed = ring if packed is None else jnp.where(lane >= at, ring, packed)
                at += 2 * WINDOW[level]
            pack_s[j, r] = packed
        return carry

    lax.fori_loop(0, strip_w // 16, pack_rows, 0)
    for n in (4, 2, 3):
        start(rises[n])

    zero = jnp.zeros((RIM, LANES), jnp.float32)

    def clear_bands(refs):
        @pl.when(b == 0)
        def _():
            for ref in refs:
                ref[low] = zero

        @pl.when(b == bands - 1)
        def _():
            for ref in refs:
                ref[high] = zero

    to_neighbours(b, bands, y_copies, "recv")
    clear_bands([wide.at[f] for f in range(7)])

    def look_up(i, carry):
        here = pl.ds(pl.multiple_of(i * 64, 8), 64)
        kind = kinds[here]
        depth = jnp.full((64, LANES), table[0], jnp.float32)
        for c in range(1, table.shape[0]):
            depth = jnp.where(kind == c, table[c], depth)
        wide[7, here] = depth
        return carry

    lax.fori_loop(0, (tile_y + 2 * RIM) // 64, look_up, 0)

    own_x = pl.ds(TOP, tile_x)
    before, after = pl.ds(PAD, RIM), pl.ds(TOP + tile_x, RIM)

    def turned(src, j):
        return src[pl.ds(j, LANES, stride=JS)].T

    def x_exchange(n, ref, depth):
        lead = (slice(None),) * (len(ref.shape) - 2)
        return [
            remote(
                ref.at[lead + (pl.ds(TOP, depth),)], ref.at[lead + (pl.ds(TOP + tile_x, depth),)],
                x_send.at[0, n], x_recv.at[0, n], along_gx(-1),
            ),
            remote(
                ref.at[lead + (pl.ds(TOP + tile_x - depth, depth),)],
                ref.at[lead + (pl.ds(TOP - depth, depth),)],
                x_send.at[1, n], x_recv.at[1, n], along_gx(1),
            ),
        ]

    x_copies = [x_exchange(n, *of) for n, of in enumerate(((dep, 26), (eta, 28), (uu, 27), (vv, 26)))]
    for j in range(JS):
        dep[j, own_x] = turned(wide.at[7], j)
    for j in range(JS):
        eta[j, own_x] = turned(wide.at[0], j)
    for k in range(3):
        for j in range(JS):
            uu[k, j, own_x] = turned(wide.at[1 + k], j)
    for k in range(3):
        for j in range(JS):
            vv[k, j, own_x] = turned(wide.at[4 + k], j)

    block = ngy * rc
    size = min(block, LANES)
    for j in range(cells_x // LANES):
        value = hm[:, j * LANES : (j + 1) * LANES].T
        for part in range(LANES // size):
            x0 = j * LANES + part * size
            group = x0 // block
            hmt[group // ngx, group % ngx, pl.ds(x0 % block, size)] = value[
                part * size : (part + 1) * size
            ]
    hm_copies = []
    for j in range(1, ngx):
        device = along_gx(j)
        hm_copies.append(
            remote(hmt.at[:, device[1]], rx.at[g], hm_send.at[j], hm_recv.at[j], device)
        )
    hm_copies.append(pltpu.make_async_copy(hmt.at[:, g], rx.at[g], own_sem.at[5]))

    def over_rows(depth, fn):
        lo = (TOP - depth) // 8 * 8
        count = -(-(TOP + tile_x + depth - lo) // TILE)
        group = max(u for u in range(1, UNROLL + 1) if count % u == 0)

        def body(i, carry):
            fn(pl.multiple_of(lo + i * TILE, 8))
            return carry

        lax.fori_loop(0, count, body, 0, unroll=group)

    def make_mask(r):
        here = pl.ds(r, TILE)
        x = r + lax.broadcasted_iota(jnp.int32, (TILE, LANES), 0)
        columns = ((x >= TOP) | (g > 0)) & ((x < TOP + tile_x) | (g < ngx - 1))
        for j in range(JS):
            at = JS * lane_of((TILE, LANES)) + j
            band = ((at >= RIM) | (b > 0)) & ((at < RIM + tile_y) | (b < bands - 1))
            mask[j, here] = (columns & band).astype(jnp.float32)

    over_rows(RIM, make_mask)

    def land(n):
        clear_bands([wide_rise.at[n]])
        if n < LEVELS:
            for j in range(JS):
                rt[n, j, own_x] = turned(wide_rise.at[n], j)
            return
        for j in range(JS):
            value = turned(wide_rise.at[n], j)
            for level in range(LEVELS):
                w, at = WINDOW[level], SHIFT[level]
                rt[level, j, pl.ds(TOP - w, w)] = value[at - w : at]
                rt[level, j, pl.ds(TOP + tile_x, w)] = value[at : at + w]

    for i, n in enumerate(order):
        finish_recv(rises[n])
        to_neighbours(b, bands, [relay[n]], "start")
        if i in X_AFTER:
            to_neighbours(g, ngx, [x_copies[m] for m in X_AFTER[i]], "start")
    for n in order:
        to_neighbours(b, bands, [relay[n]], "recv")
        land(n)

    to_neighbours(g, ngx, x_copies, "recv")
    to_neighbours(g, ngx, x_copies, "sent")
    start(hm_copies)

    def clear_columns(rows):
        nothing = jnp.zeros((JS, RIM, LANES), jnp.float32)
        dep[:, rows] = nothing + 1.0
        eta[:, rows] = nothing
        for k in range(3):
            uu[k, :, rows] = nothing
            vv[k, :, rows] = nothing
        for level in range(LEVELS):
            rt[level, :, rows] = nothing

    @pl.when(g == 0)
    def _():
        clear_columns(before)

    @pl.when(g == ngx - 1)
    def _():
        clear_columns(after)

    def invert(r):
        here = pl.ds(r, TILE)
        for j in range(JS):
            depth = dep[j, here]
            scale = mask[j, here] * SPREAD
            k = 9.0 / (depth * depth)
            i1 = 1.0 / (1.0 + 3.0 * k)
            l1 = k * i1
            i2 = 1.0 / (1.0 + 2.0 * k - k * l1)
            l2 = k * i2
            i3 = 1.0 / (1.0 + k - k * l2)
            coef[0, j, here] = l1
            coef[1, j, here] = l2
            coef[2, j, here] = i1 * scale
            coef[3, j, here] = i2 * scale
            coef[4, j, here] = i3 * scale

    over_rows(26, invert)

    def solve(j, here, v):
        l1, l2 = coef[0, j, here], coef[1, j, here]
        y2 = v[1] + l1 * v[0]
        y3 = v[2] + l2 * y2
        x3 = y3 * coef[4, j, here]
        x2 = y2 * coef[3, j, here] + l2 * x3
        x1 = v[0] * coef[2, j, here] + l1 * x2
        return x1, x2, x3

    def ring(ref, here):
        c = [ref[j, here] for j in range(JS)]
        return [turn(c[-1], 1)] + c + [turn(c[0], -1)]

    def predict(depth):
        def rows_of(r):
            here, up, down = pl.ds(r, TILE), pl.ds(r + 1, TILE), pl.ds(r - 1, TILE)
            c = ring(eta, here)
            for j in range(JS):
                push = mask[j, here] * (0.5 * GRAVITY_PUSH)
                ge = push * (eta[j, up] - eta[j, down])
                gn = push * (c[j + 2] - c[j])
                for k in range(3):
                    uu[k, j, here] = uu[k, j, here] - ge
                    vv[k, j, here] = vv[k, j, here] - gn

        over_rows(depth, rows_of)

    def source(depth, level):
        def rows_of(r):
            here, up, down = pl.ds(r, TILE), pl.ds(r + 1, TILE), pl.ds(r - 1, TILE)
            c = [ring(vv.at[k], here) for k in range(3)]
            for j in range(JS):
                rise = rt[level, j, here]
                v = []
                for k in range(3):
                    spread = (uu[k, j, up] - uu[k, j, down]) + (c[k][j + 2] - c[k][j])
                    v.append((4.0 * SOURCE * LAYER_SHARE[k]) * rise - 2.0 * spread)
                    ss[k, j, here] = v[k]
                if level == 0:
                    for k, value in enumerate(solve(j, here, v)):
                        pb[k, j, here] = value

        over_rows(depth, rows_of)

    def sweep(depth, old, new):
        def rows_of(r):
            here, up, down = pl.ds(r, TILE), pl.ds(r + 1, TILE), pl.ds(r - 1, TILE)
            c = [ring(old.at[k], here) for k in range(3)]
            for j in range(JS):
                v = []
                for k in range(3):
                    v.append(
                        (ss[k, j, here] + (c[k][j + 2] + c[k][j]))
                        + (old[k, j, up] + old[k, j, down])
                    )
                for k, value in enumerate(solve(j, here, v)):
                    new[k, j, here] = value

        over_rows(depth, rows_of)

    def correct(depth, level):
        def rows_of(r):
            here, up, down = pl.ds(r, TILE), pl.ds(r + 1, TILE), pl.ds(r - 1, TILE)
            c = [ring(pa.at[k], here) for k in range(3)]
            for j in range(JS):
                push = mask[j, here] * (0.5 * SPREAD)
                for k in range(3):
                    uu[k, j, here] = uu[k, j, here] - push * (pa[k, j, up] - pa[k, j, down])
                    vv[k, j, here] = vv[k, j, here] - push * (c[k][j + 2] - c[k][j])
                if level < LEVELS - 1:
                    low_layer = c[2][j + 1] * (1.0 / LEVELS)
                    qq[j, here] = low_layer if level == 0 else qq[j, here] + low_layer

        over_rows(depth, rows_of)

    def raise_surface(depth, level):
        def rows_of(r):
            here, up, down = pl.ds(r, TILE), pl.ds(r + 1, TILE), pl.ds(r - 1, TILE)
            c = [
                vv[0, j, here] + vv[1, j, here] + vv[2, j, here] for j in range(JS)
            ]
            c = [turn(c[-1], 1)] + c + [turn(c[0], -1)]
            for j in range(JS):
                push = mask[j, here] * (0.5 * SURFACE_STEP)
                total = (uu[0, j, up] + uu[1, j, up] + uu[2, j, up]) - (
                    uu[0, j, down] + uu[1, j, down] + uu[2, j, down]
                )
                eta[j, here] = (
                    eta[j, here] - push * (total + (c[j + 2] - c[j])) + rt[level, j, here]
                )

        over_rows(depth, rows_of)

    def begin(level):
        rim = 7 * (LEVELS - 1 - level)
        predict(rim + 6)
        source(rim + 5, level)
        if level > 0:
            sweep(rim + 5, pa, pb)
        sweep(rim + 4, pb, pa)
        sweep(rim + 3, pa, pb)
        sweep(rim + 2, pb, pa)

    def step(level):
        rim = 7 * (LEVELS - 1 - level)
        begin(level)
        correct(rim + 1, level)
        raise_surface(rim, level)

    step(0)
    step(1)

    finish_recv(hm_copies)
    lane64 = lane_of((block, LANES)) < 64
    for part in range(nsec):
        for p in range(ngx // 2):
            one, two = rx[2 * p, part], rx[2 * p + 1, part]
            columns = pl.ds(p * LANES, LANES)
            hh[0, part, :, columns] = jnp.where(lane64, one, turn(two, 64))
            hh[1, part, :, columns] = jnp.where(lane64, turn(one, 64), two)
    band_columns = pl.ds(pl.multiple_of(b * tile_y, LANES), tile_y)
    h2_copies = []
    for which, out in enumerate((thick_out, mom_out)):
        for j in range(1, bands):
            device = along_band(j)
            h2_copies.append(
                remote(
                    hh.at[which, device[0], pl.ds(pl.multiple_of(device[2] * rc, 8), rc)],
                    out.at[:, band_columns],
                    h2_send.at[which, j], h2_recv.at[which, j], device,
                )
            )
    for which, out in enumerate((thick_out, mom_out)):
        h2_copies.append(
            pltpu.make_async_copy(
                hh.at[which, s, pl.ds(pl.multiple_of(y * rc, 8), rc)],
                out.at[:, band_columns],
                own_sem.at[6 + which],
            )
        )
    start(h2_copies)

    step(2)

    def turn_back(n, ref):
        for j in range(JS):
            back[n, pl.ds(j, LANES, stride=JS)] = ref[j, own_x].T

    begin(LEVELS - 1)
    for j in range(JS):
        back[4, pl.ds(j, LANES, stride=JS)] = (
            qq[j, own_x] + pa[2, j, own_x] * (1.0 / LEVELS)
        ).T
    b_copies = []
    columns = pl.ds(pl.multiple_of(g * LANES, LANES), LANES)
    for j in range(1, ngx):
        device = along_gx(j)
        b_copies.append(
            remote(
                back.at[4, strip_rows(device[1])], bottom_out.at[0, 0, :, columns],
                b_send.at[j], b_recv.at[j], device,
            )
        )
    b_copies.append(
        pltpu.make_async_copy(
            back.at[4, strip_rows(g)], bottom_out.at[0, 0, :, columns], own_sem.at[8]
        )
    )
    start(b_copies)
    correct(1, LEVELS - 1)
    for k in range(3):
        turn_back(1 + k, pa.at[k])
    outs = [
        pltpu.make_async_copy(back.at[pl.ds(1, 3), own_rows], press_out, out_sem.at[1]),
        pltpu.make_async_copy(back.at[0, own_rows], surf_out, out_sem.at[0]),
    ]
    outs[0].start()
    raise_surface(0, LEVELS - 1)
    turn_back(0, eta)
    outs[1].start()
    finish_recv(b_copies)
    for copy in h2_copies[:-2]:
        copy.wait_recv()
    for copy in h2_copies[-2:] + outs:
        copy.wait()
    for copies in rises + [hm_copies, b_copies]:
        for copy in copies[:-1]:
            copy.wait_send()
    to_neighbours(b, bands, relay + y_copies, "sent")
    for copy in h2_copies[:-2]:
        copy.wait_send()


def write_results(*refs):
    count = (len(refs) - 2) // 3
    given, results, held = refs[:count], refs[count : 2 * count], refs[2 * count : 3 * count]
    in_sem, out_sem = refs[3 * count :]
    ins = [pltpu.make_async_copy(given[n], held[n], in_sem.at[n]) for n in range(count)]
    outs = [pltpu.make_async_copy(held[n], results[n], out_sem.at[n]) for n in range(count)]
    for copy in ins:
        copy.start()
    for n in range(count):
        ins[n].wait()
        outs[n].start()
    for copy in outs:
        copy.wait()


def shards(
    slide_thickness, footprint, slide_momentum, bed_friction, surface, flux_x, flux_y,
    bathy_class, depth_table,
):
    nsec, ngx, ngy = (lax.axis_size(a) for a in ("sec", "gx", "gy"))
    _, _, strip_w, cells_x = slide_thickness.shape
    tile_y, tile_x = surface.shape
    assert tile_x == LANES and strip_w * 2 == LANES and strip_w * ngx == tile_y
    rc = cells_x // (nsec * ngx * ngy)
    bands = nsec * ngy
    x_rows = tile_x + 2 * TOP + 16
    f32 = jnp.float32
    one = (JS, x_rows, LANES)
    three = (3,) + one
    wide_rows = JS * LANES
    results = (
        jax.ShapeDtypeStruct(surface.shape, f32),
        jax.ShapeDtypeStruct(flux_x.shape, f32),
        jax.ShapeDtypeStruct(slide_thickness.shape, f32),
        jax.ShapeDtypeStruct((rc, tile_y * bands), f32),
        jax.ShapeDtypeStruct((rc, tile_y * bands), f32),
    )
    dma = pltpu.SemaphoreType.DMA
    anywhere = pl.BlockSpec(memory_space=pl.ANY)
    made = pl.pallas_call(
        functools.partial(kernel, (nsec, ngx, ngy, tile_y, strip_w, cells_x, rc)),
        out_shape=results,
        in_specs=[anywhere] * 8 + [pl.BlockSpec(memory_space=pltpu.SMEM)],
        out_specs=(anywhere,) * 5,
        scratch_shapes=[
            pltpu.VMEM((3, strip_w, cells_x), f32),
            pltpu.VMEM((strip_w, cells_x), jnp.int32),
            pltpu.VMEM((LEVELS, ngx, strip_w, LANES), f32),
            pltpu.VMEM((ngx, strip_w, LANES), f32),
            pltpu.VMEM((2 * strip_w, cells_x), f32),
            pltpu.VMEM((nsec, ngx, ngy * rc, LANES), f32),
            pltpu.VMEM((ngx, nsec, ngy * rc, LANES), f32),
            pltpu.VMEM((2, nsec, ngy * rc, tile_y), f32),
            pltpu.VMEM((8, wide_rows, LANES), f32),
            pltpu.VMEM((tile_y + 2 * RIM, LANES), jnp.int32),
            pltpu.VMEM((LEVELS + 1, wide_rows, LANES), f32),
            pltpu.VMEM(one, f32),
            pltpu.VMEM(three, f32),
            pltpu.VMEM(three, f32),
            pltpu.VMEM(one, f32),
            pltpu.VMEM(three, f32),
            pltpu.VMEM(three, f32),
            pltpu.VMEM(three, f32),
            pltpu.VMEM((5,) + one, f32),
            pltpu.VMEM(one, f32),
            pltpu.VMEM(one, f32),
            pltpu.VMEM((LEVELS,) + one, f32),
            pltpu.VMEM((5, wide_rows, LANES), f32),
            dma((8,)),
            dma((2,)),
            dma((2, 4)), dma((2, 4)),
            dma((LEVELS + 1, ngx)), dma((LEVELS + 1, ngx)),
            dma((2, LEVELS + 1)), dma((2, LEVELS + 1)),
            dma((2, 4)), dma((2, 4)),
            dma((ngx,)), dma((ngx,)),
            dma((2, bands)), dma((2, bands)),
            dma((ngx,)), dma((ngx,)),
            dma((9,)),
        ],
        compiler_params=pltpu.CompilerParams(
            collective_id=0, has_side_effects=True, vmem_limit_bytes=56 * 2**20
        ),
    )(
        slide_thickness, footprint, slide_momentum, bed_friction, surface, flux_x, flux_y,
        bathy_class, depth_table,
    )
    return pl.pallas_call(
        write_results,
        out_shape=results,
        in_specs=[anywhere] * 5,
        out_specs=(anywhere,) * 5,
        scratch_shapes=[pltpu.VMEM(r.shape, f32) for r in results] + [dma((5,)), dma((5,))],
    )(*made)


def solution(mesh):
    strips = P(("sec", "gy"), "gx", None, None)
    tiles = P(("sec", "gy"), "gx")
    layers = P(None, ("sec", "gy"), "gx")
    turned = P(("sec", "gx", "gy"), None)
    return jax.shard_map(
        shards,
        mesh=mesh,
        in_specs=(strips,) * 4 + (tiles, layers, layers, tiles, P()),
        out_specs=(tiles, layers, strips, turned, turned),
        check_vma=False,
    )
```

```python
import functools

import jax
import jax.numpy as jnp
from jax import lax
from jax.experimental import pallas as pl
from jax.experimental.pallas import tpu as pltpu
from jax.sharding import PartitionSpec as P

LEVELS = 4
SWEEPS = 4
SPREAD = 0.25
GRAVITY_PUSH = 0.4
SOURCE = 2.0
SURFACE_STEP = 0.2
COURANT = 0.25
SLOPE_PULL = 0.5
LAYER_SHARE = (0.2, 0.3, 0.5)

LANES = 128
JS = 5
RIM = 32
TILE = 64
PAD = 8
TOP = PAD + RIM
WINDOW = (26, 19, 12, 5)
X_AFTER = {0: (0, 1), 2: (2,), 4: (3,)}
SHIFT = (26, 71, 102, 119)


def lane_of(shape):
    return lax.broadcasted_iota(jnp.int32, shape, len(shape) - 1)


def turn(value, shift):
    shift = shift % LANES
    return value if shift == 0 else pltpu.roll(value, shift, 1)


def slide_step(h, m, f, first, last):
    width = h.shape[1]

    def lo(v):
        return jnp.where(first, 0.0, pltpu.roll(v, 1, 1))

    def hi(v):
        return jnp.where(last, 0.0, pltpu.roll(v, width - 1, 1))

    u = m / (1.0 + jnp.abs(h))
    fm = m * u + 0.5 * h * h
    m_lo, m_hi = lo(m), hi(m)
    new_h = 0.5 * (lo(h) + hi(h)) - 0.5 * COURANT * (m_hi - m_lo)
    drag = f * h * u / jnp.sqrt(u * u + 1.0)
    new_m = (
        0.5 * (m_lo + m_hi)
        - 0.5 * COURANT * (hi(fm) - lo(fm))
        + COURANT * (SLOPE_PULL * h - drag)
    )
    return new_h, new_m


def kernel(
    dims,
    thick_in, foot_in, mom_in, fric_in, surf_in, fx_in, fy_in, bathy_in, table,
    surf_out, press_out, bottom_out, thick_out, mom_out,
    sl, foot, rise_s, pack_s, hm, hmt, rx, hh,
    wide, kinds, wide_rise,
    xd, xe, xu, xv, eta, uu, vv, dep, pa, pb, ss, coef, mask, qq, rt, back,
    load_sem, out_sem, ys_send, ys_recv, rise_send, rise_recv, rl_send, rl_recv,
    x_send, x_recv, hm_send, hm_recv, h2_send, h2_recv, b_send, b_recv, own_sem,
):
    nsec, ngx, ngy, tile_y, strip_w, cells_x, rc = dims
    bands = nsec * ngy
    tile_x = LANES
    s, g, y = lax.axis_index("sec"), lax.axis_index("gx"), lax.axis_index("gy")
    b = s * ngy + y

    def along_gx(j):
        return (s, lax.rem(g + j + ngx, ngx), y)

    def along_band(j):
        other = lax.rem(b + j + bands, bands)
        return (other // ngy, g, lax.rem(other, ngy))

    def remote(src, dst, send, recv, device):
        return pltpu.make_async_remote_copy(
            src_ref=src, dst_ref=dst, send_sem=send, recv_sem=recv,
            device_id=device, device_id_type=pl.DeviceIdType.MESH,
        )

    def start(copies):
        for copy in copies:
            copy.start()

    def to_neighbours(at, count, pairs, what):
        @pl.when(at > 0)
        def _():
            for pair in pairs:
                if what == "recv":
                    pair[1].wait_recv()
                else:
                    pair[0].start() if what == "start" else pair[0].wait_send()

        @pl.when(at < count - 1)
        def _():
            for pair in pairs:
                if what == "recv":
                    pair[0].wait_recv()
                else:
                    pair[1].start() if what == "start" else pair[1].wait_send()

    def finish_recv(copies):
        for copy in copies[:-1]:
            copy.wait_recv()
        copies[-1].wait()

    barrier = pltpu.get_barrier_semaphore()
    partners = [along_gx(j) for j in range(1, ngx)] + [along_band(j) for j in range(1, bands)]
    for device in partners:
        pl.semaphore_signal(barrier, inc=1, device_id=device, device_id_type=pl.DeviceIdType.MESH)

    own_rows = pl.ds(RIM, tile_y)
    loads = [
        pltpu.make_async_copy(thick_in.at[0, 0], sl.at[0], load_sem.at[0]),
        pltpu.make_async_copy(foot_in.at[0, 0], foot, load_sem.at[1]),
        pltpu.make_async_copy(mom_in.at[0, 0], sl.at[1], load_sem.at[2]),
        pltpu.make_async_copy(fric_in.at[0, 0], sl.at[2], load_sem.at[3]),
        pltpu.make_async_copy(surf_in, wide.at[0, own_rows], load_sem.at[4]),
        pltpu.make_async_copy(fx_in, wide.at[pl.ds(1, 3), own_rows], load_sem.at[5]),
        pltpu.make_async_copy(fy_in, wide.at[pl.ds(4, 3), own_rows], load_sem.at[6]),
        pltpu.make_async_copy(bathy_in, kinds.at[own_rows], load_sem.at[7]),
    ]
    start(loads)

    for copy in loads[:4]:
        copy.wait()

    def slide_rows(i, carry):
        r = pl.ds(pl.multiple_of(i * 8, 8), 8)
        lane = lane_of((8, cells_x))
        first, last = lane == 0, lane == cells_x - 1
        h = sl[0, r] * foot[r].astype(jnp.float32)
        m, f = sl[1, r], sl[2, r]
        for level in range(LEVELS):
            new_h, m = slide_step(h, m, f, first, last)
            rise = new_h - h
            for j in range(ngx):
                rise_s[level, j, r] = rise[:, j * LANES : (j + 1) * LANES]
            h = new_h
        hm[r] = h
        hm[pl.ds(pl.multiple_of(i * 8 + strip_w, 8), 8)] = m
        return carry

    lax.fori_loop(0, strip_w // 8, slide_rows, 0)

    pl.semaphore_wait(barrier, len(partners))

    for copy in loads[4:]:
        copy.wait()
    low, high = pl.ds(0, RIM), pl.ds(RIM + tile_y, RIM)
    first_rows, last_rows = pl.ds(RIM, RIM), pl.ds(tile_y, RIM)
    y_copies = []
    for n, of in enumerate((lambda r: wide.at[pl.ds(0, 7), r], lambda r: kinds.at[r])):
        y_copies.append(
            (
                remote(of(first_rows), of(high), ys_send.at[0, n], ys_recv.at[0, n], along_band(-1)),
                remote(of(last_rows), of(low), ys_send.at[1, n], ys_recv.at[1, n], along_band(1)),
            )
        )
    to_neighbours(b, bands, y_copies, "start")

    def strip_rows(j):
        return pl.ds(pl.multiple_of(RIM + j * strip_w, 8), strip_w)

    def rise_copies(n, src):
        copies = []
        for j in range(1, ngx):
            device = along_gx(j)
            copies.append(
                remote(
                    src(device[1]), wide_rise.at[n, strip_rows(g)],
                    rise_send.at[n, j], rise_recv.at[n, j], device,
                )
            )
        own = pltpu.make_async_copy(src(g), wide_rise.at[n, strip_rows(g)], own_sem.at[n])
        return copies + [own]

    rises = [rise_copies(n, lambda j, n=n: rise_s.at[n, j]) for n in range(LEVELS)]
    rises.append(rise_copies(LEVELS, lambda j: pack_s.at[j]))
    relay = []
    for n in range(LEVELS + 1):
        ref = wide_rise.at[n]
        relay.append(
            [
                remote(
                    ref.at[pl.ds(RIM, RIM)], ref.at[high],
                    rl_send.at[0, n], rl_recv.at[0, n], along_band(-1),
                ),
                remote(
                    ref.at[pl.ds(tile_y, RIM)], ref.at[low],
                    rl_send.at[1, n], rl_recv.at[1, n], along_band(1),
                ),
            ]
        )
    order = (0, 1, 4, 2, 3)
    start(rises[0])
    start(rises[1])

    def pack_rows(i, carry):
        r = pl.ds(pl.multiple_of(i * 16, 16), 16)
        lane = lane_of((16, LANES))
        for j in range(ngx):
            packed = None
            at = 0
            for level in range(LEVELS):
                ring = jnp.where(
                    lane < 64,
                    rise_s[level, min(j + 1, ngx - 1), r],
                    rise_s[level, max(j - 1, 0), r],
                )
                ring = turn(ring, SHIFT[level])
                packed = ring if packed is None else jnp.where(lane >= at, ring, packed)
                at += 2 * WINDOW[level]
            pack_s[j, r] = packed
        return carry

    lax.fori_loop(0, strip_w // 16, pack_rows, 0)
    for n in (4, 2, 3):
        start(rises[n])

    zero = jnp.zeros((RIM, LANES), jnp.float32)

    def clear_bands(refs):
        @pl.when(b == 0)
        def _():
            for ref in refs:
                ref[low] = zero

        @pl.when(b == bands - 1)
        def _():
            for ref in refs:
                ref[high] = zero

    to_neighbours(b, bands, y_copies, "recv")
    clear_bands([wide.at[f] for f in range(7)])

    def look_up(i, carry):
        here = pl.ds(pl.multiple_of(i * 64, 8), 64)
        kind = kinds[here]
        depth = jnp.full((64, LANES), table[0], jnp.float32)
        for c in range(1, table.shape[0]):
            depth = jnp.where(kind == c, table[c], depth)
        wide[7, here] = depth
        return carry

    lax.fori_loop(0, (tile_y + 2 * RIM) // 64, look_up, 0)

    own_x = pl.ds(TOP, tile_x)
    before, after = pl.ds(PAD, RIM), pl.ds(TOP + tile_x, RIM)

    def turned(src, j):
        return src[pl.ds(j, LANES, stride=JS)].T

    def x_exchange(n, kept, ref, depth):
        lead = (slice(None),) * (len(ref.shape) - 2)
        return (
            remote(
                kept.at[(0,) + lead + (pl.ds(0, depth),)],
                ref.at[lead + (pl.ds(TOP + tile_x, depth),)],
                x_send.at[0, n], x_recv.at[0, n], along_gx(-1),
            ),
            remote(
                kept.at[(1,) + lead + (pl.ds(RIM - depth, depth),)],
                ref.at[lead + (pl.ds(TOP - depth, depth),)],
                x_send.at[1, n], x_recv.at[1, n], along_gx(1),
            ),
        )

    x_copies = [
        x_exchange(n, *of)
        for n, of in enumerate(((xd, dep, 26), (xe, eta, 28), (xu, uu, 27), (xv, vv, 26)))
    ]
    for j in range(JS):
        for f, kept, ref in ((7, xd, dep), (0, xe, eta)):
            value = turned(wide.at[f], j)
            ref[j, own_x] = value
            kept[0, j] = value[:RIM]
            kept[1, j] = value[tile_x - RIM :]
        for k in range(3):
            for f, kept, ref in ((1 + k, xu, uu), (4 + k, xv, vv)):
                value = turned(wide.at[f], j)
                ref[k, j, own_x] = value
                kept[0, k, j] = value[:RIM]
                kept[1, k, j] = value[tile_x - RIM :]

    block = ngy * rc
    size = min(block, LANES)
    for j in range(cells_x // LANES):
        value = hm[:, j * LANES : (j + 1) * LANES].T
        for part in range(LANES // size):
            x0 = j * LANES + part * size
            group = x0 // block
            hmt[group // ngx, group % ngx, pl.ds(x0 % block, size)] = value[
                part * size : (part + 1) * size
            ]
    hm_copies = []
    for j in range(1, ngx):
        device = along_gx(j)
        hm_copies.append(
            remote(hmt.at[:, device[1]], rx.at[g], hm_send.at[j], hm_recv.at[j], device)
        )
    hm_copies.append(pltpu.make_async_copy(hmt.at[:, g], rx.at[g], own_sem.at[5]))

    def over_rows(depth, fn, part=None, inner=0):
        lo = TOP - depth
        if part is None:
            lo = lo // 8 * 8
            tile, stride = TILE, TILE
            count = -(-(TOP + tile_x + depth - lo) // TILE)
        elif part == "inner":
            lo = TOP + inner
            count = 2
            tile = stride = tile_x // 2 - inner
        else:
            count = 2
            tile = depth + inner
            stride = tile_x - inner + depth

        def body(i, carry):
            start_row = lo + i * stride
            if part is None:
                start_row = pl.multiple_of(start_row, 8)
            fn(start_row, tile)
            return carry

        lax.fori_loop(0, count, body, 0)

    def make_mask(r, tile):
        here = pl.ds(r, tile)
        x = r + lax.broadcasted_iota(jnp.int32, (tile, LANES), 0)
        columns = ((x >= TOP) | (g > 0)) & ((x < TOP + tile_x) | (g < ngx - 1))
        for j in range(JS):
            at = JS * lane_of((tile, LANES)) + j
            band = ((at >= RIM) | (b > 0)) & ((at < RIM + tile_y) | (b < bands - 1))
            mask[j, here] = (columns & band).astype(jnp.float32)

    over_rows(RIM, make_mask)

    def land(n):
        clear_bands([wide_rise.at[n]])
        if n < LEVELS:
            for j in range(JS):
                rt[n, j, own_x] = turned(wide_rise.at[n], j)
            return
        for j in range(JS):
            value = turned(wide_rise.at[n], j)
            for level in range(LEVELS):
                w, at = WINDOW[level], SHIFT[level]
                rt[level, j, pl.ds(TOP - w, w)] = value[at - w : at]
                rt[level, j, pl.ds(TOP + tile_x, w)] = value[at : at + w]

    for i, n in enumerate(order):
        finish_recv(rises[n])
        to_neighbours(b, bands, [relay[n]], "start")
        if i in X_AFTER:
            to_neighbours(g, ngx, [x_copies[m] for m in X_AFTER[i]], "start")
    for n in order:
        to_neighbours(b, bands, [relay[n]], "recv")
        land(n)

    to_neighbours(g, ngx, x_copies[:1], "recv")

    @pl.when(g == 0)
    def _():
        dep[:, before] = jnp.ones((JS, RIM, LANES), jnp.float32)

    @pl.when(g == ngx - 1)
    def _():
        dep[:, after] = jnp.ones((JS, RIM, LANES), jnp.float32)

    def invert(r, tile):
        here = pl.ds(r, tile)
        for j in range(JS):
            depth = dep[j, here]
            scale = mask[j, here] * SPREAD
            k = 9.0 / (depth * depth)
            i1 = 1.0 / (1.0 + 3.0 * k)
            l1 = k * i1
            i2 = 1.0 / (1.0 + 2.0 * k - k * l1)
            l2 = k * i2
            i3 = 1.0 / (1.0 + k - k * l2)
            coef[0, j, here] = l1
            coef[1, j, here] = l2
            coef[2, j, here] = i1 * scale
            coef[3, j, here] = i2 * scale
            coef[4, j, here] = i3 * scale

    over_rows(26, invert)


    def solve(j, here, v):
        l1, l2 = coef[0, j, here], coef[1, j, here]
        y2 = v[1] + l1 * v[0]
        y3 = v[2] + l2 * y2
        x3 = y3 * coef[4, j, here]
        x2 = y2 * coef[3, j, here] + l2 * x3
        x1 = v[0] * coef[2, j, here] + l1 * x2
        return x1, x2, x3

    def ring(ref, here):
        c = [ref[j, here] for j in range(JS)]
        return [turn(c[-1], 1)] + c + [turn(c[0], -1)]

    def predict(depth, *part):
        def rows_of(r, tile):
            here, up, down = pl.ds(r, tile), pl.ds(r + 1, tile), pl.ds(r - 1, tile)
            c = ring(eta, here)
            for j in range(JS):
                push = mask[j, here] * (0.5 * GRAVITY_PUSH)
                ge = push * (eta[j, up] - eta[j, down])
                gn = push * (c[j + 2] - c[j])
                for k in range(3):
                    uu[k, j, here] = uu[k, j, here] - ge
                    vv[k, j, here] = vv[k, j, here] - gn

        over_rows(depth, rows_of, *part)

    def source(depth, level, *part):
        def rows_of(r, tile):
            here, up, down = pl.ds(r, tile), pl.ds(r + 1, tile), pl.ds(r - 1, tile)
            c = [ring(vv.at[k], here) for k in range(3)]
            for j in range(JS):
                rise = rt[level, j, here]
                v = []
                for k in range(3):
                    spread = (uu[k, j, up] - uu[k, j, down]) + (c[k][j + 2] - c[k][j])
                    v.append((4.0 * SOURCE * LAYER_SHARE[k]) * rise - 2.0 * spread)
                    ss[k, j, here] = v[k]
                if level == 0:
                    for k, value in enumerate(solve(j, here, v)):
                        pb[k, j, here] = value

        over_rows(depth, rows_of, *part)

    def sweep(depth, old, new, *part):
        def rows_of(r, tile):
            here, up, down = pl.ds(r, tile), pl.ds(r + 1, tile), pl.ds(r - 1, tile)
            c = [ring(old.at[k], here) for k in range(3)]
            for j in range(JS):
                v = []
                for k in range(3):
                    v.append(
                        (ss[k, j, here] + (c[k][j + 2] + c[k][j]))
                        + (old[k, j, up] + old[k, j, down])
                    )
                for k, value in enumerate(solve(j, here, v)):
                    new[k, j, here] = value

        over_rows(depth, rows_of, *part)

    def correct(depth, level, *part):
        def rows_of(r, tile):
            here, up, down = pl.ds(r, tile), pl.ds(r + 1, tile), pl.ds(r - 1, tile)
            c = [ring(pa.at[k], here) for k in range(3)]
            for j in range(JS):
                push = mask[j, here] * (0.5 * SPREAD)
                for k in range(3):
                    uu[k, j, here] = uu[k, j, here] - push * (pa[k, j, up] - pa[k, j, down])
                    vv[k, j, here] = vv[k, j, here] - push * (c[k][j + 2] - c[k][j])
                if level < LEVELS - 1:
                    low_layer = c[2][j + 1] * (1.0 / LEVELS)
                    qq[j, here] = low_layer if level == 0 else qq[j, here] + low_layer

        over_rows(depth, rows_of, *part)

    def raise_surface(depth, level, *part):
        def rows_of(r, tile):
            here, up, down = pl.ds(r, tile), pl.ds(r + 1, tile), pl.ds(r - 1, tile)
            c = [
                vv[0, j, here] + vv[1, j, here] + vv[2, j, here] for j in range(JS)
            ]
            c = [turn(c[-1], 1)] + c + [turn(c[0], -1)]
            for j in range(JS):
                push = mask[j, here] * (0.5 * SURFACE_STEP)
                total = (uu[0, j, up] + uu[1, j, up] + uu[2, j, up]) - (
                    uu[0, j, down] + uu[1, j, down] + uu[2, j, down]
                )
                eta[j, here] = (
                    eta[j, here] - push * (total + (c[j + 2] - c[j])) + rt[level, j, here]
                )

        over_rows(depth, rows_of, *part)

    def begin(level, part=None):
        rim = 7 * (LEVELS - 1 - level)
        at = 7 * level + 1
        predict(rim + 6, part, at)
        source(rim + 5, level, part, at + 1)
        if level > 0:
            sweep(rim + 5, pa, pb, part, at + 1)
        sweep(rim + 4, pb, pa, part, at + 2)
        sweep(rim + 3, pa, pb, part, at + 3)
        sweep(rim + 2, pb, pa, part, at + 4)

    def step(level, part=None):
        rim = 7 * (LEVELS - 1 - level)
        at = 7 * level + 1
        begin(level, part)
        correct(rim + 1, level, part, at + 5)
        raise_surface(rim, level, part, at + 6)

    for level in range(2):
        step(level, "inner")
    to_neighbours(g, ngx, x_copies[1:], "recv")
    start(hm_copies)

    def clear_columns(rows):
        nothing = jnp.zeros((JS, RIM, LANES), jnp.float32)
        eta[:, rows] = nothing
        for k in range(3):
            uu[k, :, rows] = nothing
            vv[k, :, rows] = nothing
        for level in range(LEVELS):
            rt[level, :, rows] = nothing

    @pl.when(g == 0)
    def _():
        clear_columns(before)

    @pl.when(g == ngx - 1)
    def _():
        clear_columns(after)
    for level in range(2):
        step(level, "outer")

    step(2)

    finish_recv(hm_copies)
    lane64 = lane_of((block, LANES)) < 64
    for part in range(nsec):
        for p in range(ngx // 2):
            one, two = rx[2 * p, part], rx[2 * p + 1, part]
            columns = pl.ds(p * LANES, LANES)
            hh[0, part, :, columns] = jnp.where(lane64, one, turn(two, 64))
            hh[1, part, :, columns] = jnp.where(lane64, turn(one, 64), two)
    band_columns = pl.ds(pl.multiple_of(b * tile_y, LANES), tile_y)
    h2_copies = []
    for which, out in enumerate((thick_out, mom_out)):
        for j in range(1, bands):
            device = along_band(j)
            h2_copies.append(
                remote(
                    hh.at[which, device[0], pl.ds(pl.multiple_of(device[2] * rc, 8), rc)],
                    out.at[:, band_columns],
                    h2_send.at[which, j], h2_recv.at[which, j], device,
                )
            )
    for which, out in enumerate((thick_out, mom_out)):
        h2_copies.append(
            pltpu.make_async_copy(
                hh.at[which, s, pl.ds(pl.multiple_of(y * rc, 8), rc)],
                out.at[:, band_columns],
                own_sem.at[6 + which],
            )
        )
    start(h2_copies)

    def turn_back(n, ref):
        for j in range(JS):
            back[n, pl.ds(j, LANES, stride=JS)] = ref[j, own_x].T

    begin(LEVELS - 1)
    for j in range(JS):
        back[4, pl.ds(j, LANES, stride=JS)] = (
            qq[j, own_x] + pa[2, j, own_x] * (1.0 / LEVELS)
        ).T
    b_copies = []
    columns = pl.ds(pl.multiple_of(g * LANES, LANES), LANES)
    for j in range(1, ngx):
        device = along_gx(j)
        b_copies.append(
            remote(
                back.at[4, strip_rows(device[1])], bottom_out.at[0, 0, :, columns],
                b_send.at[j], b_recv.at[j], device,
            )
        )
    b_copies.append(
        pltpu.make_async_copy(
            back.at[4, strip_rows(g)], bottom_out.at[0, 0, :, columns], own_sem.at[8]
        )
    )
    start(b_copies)
    correct(1, LEVELS - 1)
    for k in range(3):
        turn_back(1 + k, pa.at[k])
    outs = [
        pltpu.make_async_copy(back.at[pl.ds(1, 3), own_rows], press_out, out_sem.at[1]),
        pltpu.make_async_copy(back.at[0, own_rows], surf_out, out_sem.at[0]),
    ]
    outs[0].start()
    raise_surface(0, LEVELS - 1)
    turn_back(0, eta)
    outs[1].start()
    finish_recv(b_copies)
    for copy in h2_copies[:-2]:
        copy.wait_recv()
    for copy in h2_copies[-2:] + outs:
        copy.wait()
    for copies in rises + [hm_copies, b_copies]:
        for copy in copies[:-1]:
            copy.wait_send()
    to_neighbours(b, bands, relay + y_copies, "sent")
    to_neighbours(g, ngx, x_copies, "sent")
    for copy in h2_copies[:-2]:
        copy.wait_send()


def write_results(*refs):
    count = (len(refs) - 2) // 3
    given, results, held = refs[:count], refs[count : 2 * count], refs[2 * count : 3 * count]
    in_sem, out_sem = refs[3 * count :]
    ins = [pltpu.make_async_copy(given[n], held[n], in_sem.at[n]) for n in range(count)]
    outs = [pltpu.make_async_copy(held[n], results[n], out_sem.at[n]) for n in range(count)]
    for copy in ins:
        copy.start()
    for n in range(count):
        ins[n].wait()
        outs[n].start()
    for copy in outs:
        copy.wait()


def shards(
    slide_thickness, footprint, slide_momentum, bed_friction, surface, flux_x, flux_y,
    bathy_class, depth_table,
):
    nsec, ngx, ngy = (lax.axis_size(a) for a in ("sec", "gx", "gy"))
    _, _, strip_w, cells_x = slide_thickness.shape
    tile_y, tile_x = surface.shape
    assert tile_x == LANES and strip_w * 2 == LANES and strip_w * ngx == tile_y
    rc = cells_x // (nsec * ngx * ngy)
    bands = nsec * ngy
    x_rows = tile_x + 2 * TOP + 48
    f32 = jnp.float32
    one = (JS, x_rows, LANES)
    three = (3,) + one
    wide_rows = JS * LANES
    results = (
        jax.ShapeDtypeStruct(surface.shape, f32),
        jax.ShapeDtypeStruct(flux_x.shape, f32),
        jax.ShapeDtypeStruct(slide_thickness.shape, f32),
        jax.ShapeDtypeStruct((rc, tile_y * bands), f32),
        jax.ShapeDtypeStruct((rc, tile_y * bands), f32),
    )
    dma = pltpu.SemaphoreType.DMA
    anywhere = pl.BlockSpec(memory_space=pl.ANY)
    made = pl.pallas_call(
        functools.partial(kernel, (nsec, ngx, ngy, tile_y, strip_w, cells_x, rc)),
        out_shape=results,
        in_specs=[anywhere] * 8 + [pl.BlockSpec(memory_space=pltpu.SMEM)],
        out_specs=(anywhere,) * 5,
        scratch_shapes=[
            pltpu.VMEM((3, strip_w, cells_x), f32),
            pltpu.VMEM((strip_w, cells_x), jnp.int32),
            pltpu.VMEM((LEVELS, ngx, strip_w, LANES), f32),
            pltpu.VMEM((ngx, strip_w, LANES), f32),
            pltpu.VMEM((2 * strip_w, cells_x), f32),
            pltpu.VMEM((nsec, ngx, ngy * rc, LANES), f32),
            pltpu.VMEM((ngx, nsec, ngy * rc, LANES), f32),
            pltpu.VMEM((2, nsec, ngy * rc, tile_y), f32),
            pltpu.VMEM((8, wide_rows, LANES), f32),
            pltpu.VMEM((tile_y + 2 * RIM, LANES), jnp.int32),
            pltpu.VMEM((LEVELS + 1, wide_rows, LANES), f32),
            pltpu.VMEM((2, JS, RIM, LANES), f32),
            pltpu.VMEM((2, JS, RIM, LANES), f32),
            pltpu.VMEM((2, 3, JS, RIM, LANES), f32),
            pltpu.VMEM((2, 3, JS, RIM, LANES), f32),
            pltpu.VMEM(one, f32),
            pltpu.VMEM(three, f32),
            pltpu.VMEM(three, f32),
            pltpu.VMEM(one, f32),
            pltpu.VMEM(three, f32),
            pltpu.VMEM(three, f32),
            pltpu.VMEM(three, f32),
            pltpu.VMEM((5,) + one, f32),
            pltpu.VMEM(one, f32),
            pltpu.VMEM(one, f32),
            pltpu.VMEM((LEVELS,) + one, f32),
            pltpu.VMEM((5, wide_rows, LANES), f32),
            dma((8,)),
            dma((2,)),
            dma((2, 4)), dma((2, 4)),
            dma((LEVELS + 1, ngx)), dma((LEVELS + 1, ngx)),
            dma((2, LEVELS + 1)), dma((2, LEVELS + 1)),
            dma((2, 4)), dma((2, 4)),
            dma((ngx,)), dma((ngx,)),
            dma((2, bands)), dma((2, bands)),
            dma((ngx,)), dma((ngx,)),
            dma((9,)),
        ],
        compiler_params=pltpu.CompilerParams(
            collective_id=0, has_side_effects=True, vmem_limit_bytes=56 * 2**20
        ),
    )(
        slide_thickness, footprint, slide_momentum, bed_friction, surface, flux_x, flux_y,
        bathy_class, depth_table,
    )
    return pl.pallas_call(
        write_results,
        out_shape=results,
        in_specs=[anywhere] * 5,
        out_specs=(anywhere,) * 5,
        scratch_shapes=[pltpu.VMEM(r.shape, f32) for r in results] + [dma((5,)), dma((5,))],
    )(*made)


def solution(mesh):
    strips = P(("sec", "gy"), "gx", None, None)
    tiles = P(("sec", "gy"), "gx")
    layers = P(None, ("sec", "gy"), "gx")
    turned = P(("sec", "gx", "gy"), None)
    return jax.shard_map(
        shards,
        mesh=mesh,
        in_specs=(strips,) * 4 + (tiles, layers, layers, tiles, P()),
        out_specs=(tiles, layers, strips, turned, turned),
        check_vma=False,
    )
```

```python
import functools

import jax
import jax.numpy as jnp
from jax import lax
from jax.experimental import pallas as pl
from jax.experimental.pallas import tpu as pltpu
from jax.sharding import PartitionSpec as P

LEVELS = 4
SWEEPS = 4
SPREAD = 0.25
GRAVITY_PUSH = 0.4
SOURCE = 2.0
SURFACE_STEP = 0.2
COURANT = 0.25
SLOPE_PULL = 0.5
LAYER_SHARE = (0.2, 0.3, 0.5)

LANES = 128
JS = 5
RIM = 32
TILE = 64
PAD = 8
TOP = PAD + RIM
WINDOW = (26, 19, 12, 5)
X_AFTER = {0: (0, 1), 2: (2,), 4: (3,)}
SHIFT = (26, 71, 102, 119)


def lane_of(shape):
    return lax.broadcasted_iota(jnp.int32, shape, len(shape) - 1)


def turn(value, shift):
    shift = shift % LANES
    return value if shift == 0 else pltpu.roll(value, shift, 1)


def slide_step(h, m, f, first, last):
    width = h.shape[1]

    def lo(v):
        return jnp.where(first, 0.0, pltpu.roll(v, 1, 1))

    def hi(v):
        return jnp.where(last, 0.0, pltpu.roll(v, width - 1, 1))

    u = m / (1.0 + jnp.abs(h))
    fm = m * u + 0.5 * h * h
    m_lo, m_hi = lo(m), hi(m)
    new_h = 0.5 * (lo(h) + hi(h)) - 0.5 * COURANT * (m_hi - m_lo)
    drag = f * h * u / jnp.sqrt(u * u + 1.0)
    new_m = (
        0.5 * (m_lo + m_hi)
        - 0.5 * COURANT * (hi(fm) - lo(fm))
        + COURANT * (SLOPE_PULL * h - drag)
    )
    return new_h, new_m


def kernel(
    dims,
    thick_in, foot_in, mom_in, fric_in, surf_in, fx_in, fy_in, bathy_in, table,
    surf_out, press_out, bottom_out, thick_out, mom_out,
    sl, foot, rise_s, pack_s, hm, hmt, rx, hh,
    wide, kinds, wide_rise,
    xd, xe, xu, xv, eta, uu, vv, dep, pa, pb, ss, coef, mask, qq, rt, back,
    load_sem, out_sem, ys_send, ys_recv, rise_send, rise_recv, rl_send, rl_recv,
    x_send, x_recv, hm_send, hm_recv, h2_send, h2_recv, b_send, b_recv, own_sem,
):
    nsec, ngx, ngy, tile_y, strip_w, cells_x, rc = dims
    bands = nsec * ngy
    tile_x = LANES
    s, g, y = lax.axis_index("sec"), lax.axis_index("gx"), lax.axis_index("gy")
    b = s * ngy + y

    def along_gx(j):
        return (s, lax.rem(g + j + ngx, ngx), y)

    def along_band(j):
        other = lax.rem(b + j + bands, bands)
        return (other // ngy, g, lax.rem(other, ngy))

    def remote(src, dst, send, recv, device):
        return pltpu.make_async_remote_copy(
            src_ref=src, dst_ref=dst, send_sem=send, recv_sem=recv,
            device_id=device, device_id_type=pl.DeviceIdType.MESH,
        )

    def start(copies):
        for copy in copies:
            copy.start()

    def to_neighbours(at, count, pairs, what):
        @pl.when(at > 0)
        def _():
            for pair in pairs:
                if what == "recv":
                    pair[1].wait_recv()
                else:
                    pair[0].start() if what == "start" else pair[0].wait_send()

        @pl.when(at < count - 1)
        def _():
            for pair in pairs:
                if what == "recv":
                    pair[0].wait_recv()
                else:
                    pair[1].start() if what == "start" else pair[1].wait_send()

    def finish_recv(copies):
        for copy in copies[:-1]:
            copy.wait_recv()
        copies[-1].wait()

    barrier = pltpu.get_barrier_semaphore()
    partners = [along_gx(j) for j in range(1, ngx)] + [along_band(j) for j in range(1, bands)]
    for device in partners:
        pl.semaphore_signal(barrier, inc=1, device_id=device, device_id_type=pl.DeviceIdType.MESH)

    own_rows = pl.ds(RIM, tile_y)
    loads = [
        pltpu.make_async_copy(thick_in.at[0, 0], sl.at[0], load_sem.at[0]),
        pltpu.make_async_copy(foot_in.at[0, 0], foot, load_sem.at[1]),
        pltpu.make_async_copy(mom_in.at[0, 0], sl.at[1], load_sem.at[2]),
        pltpu.make_async_copy(fric_in.at[0, 0], sl.at[2], load_sem.at[3]),
        pltpu.make_async_copy(surf_in, wide.at[0, own_rows], load_sem.at[4]),
        pltpu.make_async_copy(fx_in, wide.at[pl.ds(1, 3), own_rows], load_sem.at[5]),
        pltpu.make_async_copy(fy_in, wide.at[pl.ds(4, 3), own_rows], load_sem.at[6]),
        pltpu.make_async_copy(bathy_in, kinds.at[own_rows], load_sem.at[7]),
    ]
    start(loads)

    for copy in loads[:4]:
        copy.wait()

    def slide_rows(i, carry):
        r = pl.ds(pl.multiple_of(i * 8, 8), 8)
        lane = lane_of((8, cells_x))
        first, last = lane == 0, lane == cells_x - 1
        h = sl[0, r] * foot[r].astype(jnp.float32)
        m, f = sl[1, r], sl[2, r]
        for level in range(LEVELS):
            new_h, m = slide_step(h, m, f, first, last)
            rise = new_h - h
            for j in range(ngx):
                rise_s[level, j, r] = rise[:, j * LANES : (j + 1) * LANES]
            h = new_h
        hm[r] = h
        hm[pl.ds(pl.multiple_of(i * 8 + strip_w, 8), 8)] = m
        return carry

    lax.fori_loop(0, strip_w // 8, slide_rows, 0)

    pl.semaphore_wait(barrier, len(partners))

    for copy in loads[4:]:
        copy.wait()
    low, high = pl.ds(0, RIM), pl.ds(RIM + tile_y, RIM)
    first_rows, last_rows = pl.ds(RIM, RIM), pl.ds(tile_y, RIM)
    y_copies = []
    for n, of in enumerate((lambda r: wide.at[pl.ds(0, 7), r], lambda r: kinds.at[r])):
        y_copies.append(
            (
                remote(of(first_rows), of(high), ys_send.at[0, n], ys_recv.at[0, n], along_band(-1)),
                remote(of(last_rows), of(low), ys_send.at[1, n], ys_recv.at[1, n], along_band(1)),
            )
        )
    to_neighbours(b, bands, y_copies, "start")

    def strip_rows(j):
        return pl.ds(pl.multiple_of(RIM + j * strip_w, 8), strip_w)

    def rise_copies(n, src):
        copies = []
        for j in range(1, ngx):
            device = along_gx(j)
            copies.append(
                remote(
                    src(device[1]), wide_rise.at[n, strip_rows(g)],
                    rise_send.at[n, j], rise_recv.at[n, j], device,
                )
            )
        own = pltpu.make_async_copy(src(g), wide_rise.at[n, strip_rows(g)], own_sem.at[n])
        return copies + [own]

    rises = [rise_copies(n, lambda j, n=n: rise_s.at[n, j]) for n in range(LEVELS)]
    rises.append(rise_copies(LEVELS, lambda j: pack_s.at[j]))
    relay = []
    for n in range(LEVELS + 1):
        ref = wide_rise.at[n]
        relay.append(
            [
                remote(
                    ref.at[pl.ds(RIM, RIM)], ref.at[high],
                    rl_send.at[0, n], rl_recv.at[0, n], along_band(-1),
                ),
                remote(
                    ref.at[pl.ds(tile_y, RIM)], ref.at[low],
                    rl_send.at[1, n], rl_recv.at[1, n], along_band(1),
                ),
            ]
        )
    order = (0, 1, 4, 2, 3)
    start(rises[0])
    start(rises[1])

    def pack_rows(i, carry):
        r = pl.ds(pl.multiple_of(i * 16, 16), 16)
        lane = lane_of((16, LANES))
        for j in range(ngx):
            packed = None
            at = 0
            for level in range(LEVELS):
                ring = jnp.where(
                    lane < 64,
                    rise_s[level, min(j + 1, ngx - 1), r],
                    rise_s[level, max(j - 1, 0), r],
                )
                ring = turn(ring, SHIFT[level])
                packed = ring if packed is None else jnp.where(lane >= at, ring, packed)
                at += 2 * WINDOW[level]
            pack_s[j, r] = packed
        return carry

    lax.fori_loop(0, strip_w // 16, pack_rows, 0)
    for n in (4, 2, 3):
        start(rises[n])

    zero = jnp.zeros((RIM, LANES), jnp.float32)

    def clear_bands(refs):
        @pl.when(b == 0)
        def _():
            for ref in refs:
                ref[low] = zero

        @pl.when(b == bands - 1)
        def _():
            for ref in refs:
                ref[high] = zero

    to_neighbours(b, bands, y_copies, "recv")
    clear_bands([wide.at[f] for f in range(7)])

    def look_up(i, carry):
        here = pl.ds(pl.multiple_of(i * 64, 8), 64)
        kind = kinds[here]
        depth = jnp.full((64, LANES), table[0], jnp.float32)
        for c in range(1, table.shape[0]):
            depth = jnp.where(kind == c, table[c], depth)
        wide[7, here] = depth
        return carry

    lax.fori_loop(0, (tile_y + 2 * RIM) // 64, look_up, 0)

    own_x = pl.ds(TOP, tile_x)
    before, after = pl.ds(PAD, RIM), pl.ds(TOP + tile_x, RIM)

    def turned(src, j):
        return src[pl.ds(j, LANES, stride=JS)].T

    def x_exchange(n, kept, ref, depth):
        lead = (slice(None),) * (len(ref.shape) - 2)
        return (
            remote(
                kept.at[(0,) + lead + (pl.ds(0, depth),)],
                ref.at[lead + (pl.ds(TOP + tile_x, depth),)],
                x_send.at[0, n], x_recv.at[0, n], along_gx(-1),
            ),
            remote(
                kept.at[(1,) + lead + (pl.ds(RIM - depth, depth),)],
                ref.at[lead + (pl.ds(TOP - depth, depth),)],
                x_send.at[1, n], x_recv.at[1, n], along_gx(1),
            ),
        )

    x_copies = [
        x_exchange(n, *of)
        for n, of in enumerate(((xd, dep, 26), (xe, eta, 28), (xu, uu, 27), (xv, vv, 26)))
    ]
    for j in range(JS):
        for f, kept, ref in ((7, xd, dep), (0, xe, eta)):
            value = turned(wide.at[f], j)
            ref[j, own_x] = value
            kept[0, j] = value[:RIM]
            kept[1, j] = value[tile_x - RIM :]
        for k in range(3):
            for f, kept, ref in ((1 + k, xu, uu), (4 + k, xv, vv)):
                value = turned(wide.at[f], j)
                ref[k, j, own_x] = value
                kept[0, k, j] = value[:RIM]
                kept[1, k, j] = value[tile_x - RIM :]

    block = ngy * rc
    size = min(block, LANES)
    for j in range(cells_x // LANES):
        value = hm[:, j * LANES : (j + 1) * LANES].T
        for part in range(LANES // size):
            x0 = j * LANES + part * size
            group = x0 // block
            hmt[group // ngx, group % ngx, pl.ds(x0 % block, size)] = value[
                part * size : (part + 1) * size
            ]
    hm_copies = []
    for j in range(1, ngx):
        device = along_gx(j)
        hm_copies.append(
            remote(hmt.at[:, device[1]], rx.at[g], hm_send.at[j], hm_recv.at[j], device)
        )
    hm_copies.append(pltpu.make_async_copy(hmt.at[:, g], rx.at[g], own_sem.at[5]))

    def over_rows(depth, fn, part=None, inner=0):
        lo = TOP - depth
        if part is None:
            lo = lo // 8 * 8
            tile, stride = TILE, TILE
            count = -(-(TOP + tile_x + depth - lo) // TILE)
        elif part == "inner":
            lo = TOP + inner
            count = 2
            tile = stride = tile_x // 2 - inner
        else:
            count = 2
            tile = depth + inner
            stride = tile_x - inner + depth

        def body(i, carry):
            start_row = lo + i * stride
            if part is None:
                start_row = pl.multiple_of(start_row, 8)
            fn(start_row, tile)
            return carry

        lax.fori_loop(0, count, body, 0)

    def make_mask(r, tile):
        here = pl.ds(r, tile)
        x = r + lax.broadcasted_iota(jnp.int32, (tile, LANES), 0)
        columns = ((x >= TOP) | (g > 0)) & ((x < TOP + tile_x) | (g < ngx - 1))
        for j in range(JS):
            at = JS * lane_of((tile, LANES)) + j
            band = ((at >= RIM) | (b > 0)) & ((at < RIM + tile_y) | (b < bands - 1))
            mask[j, here] = (columns & band).astype(jnp.float32)

    over_rows(RIM, make_mask)

    def land(n):
        clear_bands([wide_rise.at[n]])
        if n < LEVELS:
            for j in range(JS):
                rt[n, j, own_x] = turned(wide_rise.at[n], j)
            return
        for j in range(JS):
            value = turned(wide_rise.at[n], j)
            for level in range(LEVELS):
                w, at = WINDOW[level], SHIFT[level]
                rt[level, j, pl.ds(TOP - w, w)] = value[at - w : at]
                rt[level, j, pl.ds(TOP + tile_x, w)] = value[at : at + w]

    for i, n in enumerate(order):
        finish_recv(rises[n])
        to_neighbours(b, bands, [relay[n]], "start")
        if i in X_AFTER:
            to_neighbours(g, ngx, [x_copies[m] for m in X_AFTER[i]], "start")
    for n in order:
        to_neighbours(b, bands, [relay[n]], "recv")
        land(n)

    to_neighbours(g, ngx, x_copies[:1], "recv")

    @pl.when(g == 0)
    def _():
        dep[:, before] = jnp.ones((JS, RIM, LANES), jnp.float32)

    @pl.when(g == ngx - 1)
    def _():
        dep[:, after] = jnp.ones((JS, RIM, LANES), jnp.float32)

    def invert(r, tile):
        here = pl.ds(r, tile)
        for j in range(JS):
            depth = dep[j, here]
            scale = mask[j, here] * SPREAD
            k = 9.0 / (depth * depth)
            i1 = 1.0 / (1.0 + 3.0 * k)
            l1 = k * i1
            i2 = 1.0 / (1.0 + 2.0 * k - k * l1)
            l2 = k * i2
            i3 = 1.0 / (1.0 + k - k * l2)
            coef[0, j, here] = l1
            coef[1, j, here] = l2
            coef[2, j, here] = i1 * scale
            coef[3, j, here] = i2 * scale
            coef[4, j, here] = i3 * scale

    over_rows(26, invert)


    def solve(j, here, v):
        l1, l2 = coef[0, j, here], coef[1, j, here]
        y2 = v[1] + l1 * v[0]
        y3 = v[2] + l2 * y2
        x3 = y3 * coef[4, j, here]
        x2 = y2 * coef[3, j, here] + l2 * x3
        x1 = v[0] * coef[2, j, here] + l1 * x2
        return x1, x2, x3

    def ring(ref, here):
        c = [ref[j, here] for j in range(JS)]
        return [turn(c[-1], 1)] + c + [turn(c[0], -1)]

    def predict(depth, *part):
        def rows_of(r, tile):
            here, up, down = pl.ds(r, tile), pl.ds(r + 1, tile), pl.ds(r - 1, tile)
            c = ring(eta, here)
            for j in range(JS):
                push = mask[j, here] * (0.5 * GRAVITY_PUSH)
                ge = push * (eta[j, up] - eta[j, down])
                gn = push * (c[j + 2] - c[j])
                for k in range(3):
                    uu[k, j, here] = uu[k, j, here] - ge
                    vv[k, j, here] = vv[k, j, here] - gn

        over_rows(depth, rows_of, *part)

    def source(depth, level, *part):
        def rows_of(r, tile):
            here, up, down = pl.ds(r, tile), pl.ds(r + 1, tile), pl.ds(r - 1, tile)
            c = [ring(vv.at[k], here) for k in range(3)]
            for j in range(JS):
                rise = rt[level, j, here]
                v = []
                for k in range(3):
                    spread = (uu[k, j, up] - uu[k, j, down]) + (c[k][j + 2] - c[k][j])
                    v.append((4.0 * SOURCE * LAYER_SHARE[k]) * rise - 2.0 * spread)
                    ss[k, j, here] = v[k]
                if level == 0:
                    for k, value in enumerate(solve(j, here, v)):
                        pb[k, j, here] = value

        over_rows(depth, rows_of, *part)

    def sweep(depth, old, new, *part):
        def rows_of(r, tile):
            here, up, down = pl.ds(r, tile), pl.ds(r + 1, tile), pl.ds(r - 1, tile)
            c = [ring(old.at[k], here) for k in range(3)]
            for j in range(JS):
                v = []
                for k in range(3):
                    v.append(
                        (ss[k, j, here] + (c[k][j + 2] + c[k][j]))
                        + (old[k, j, up] + old[k, j, down])
                    )
                for k, value in enumerate(solve(j, here, v)):
                    new[k, j, here] = value

        over_rows(depth, rows_of, *part)

    def correct(depth, level, *part):
        def rows_of(r, tile):
            here, up, down = pl.ds(r, tile), pl.ds(r + 1, tile), pl.ds(r - 1, tile)
            c = [ring(pa.at[k], here) for k in range(3)]
            for j in range(JS):
                push = mask[j, here] * (0.5 * SPREAD)
                for k in range(3):
                    uu[k, j, here] = uu[k, j, here] - push * (pa[k, j, up] - pa[k, j, down])
                    vv[k, j, here] = vv[k, j, here] - push * (c[k][j + 2] - c[k][j])
                if level < LEVELS - 1:
                    low_layer = c[2][j + 1] * (1.0 / LEVELS)
                    qq[j, here] = low_layer if level == 0 else qq[j, here] + low_layer

        over_rows(depth, rows_of, *part)

    def raise_surface(depth, level, *part):
        def rows_of(r, tile):
            here, up, down = pl.ds(r, tile), pl.ds(r + 1, tile), pl.ds(r - 1, tile)
            c = [
                vv[0, j, here] + vv[1, j, here] + vv[2, j, here] for j in range(JS)
            ]
            c = [turn(c[-1], 1)] + c + [turn(c[0], -1)]
            for j in range(JS):
                push = mask[j, here] * (0.5 * SURFACE_STEP)
                total = (uu[0, j, up] + uu[1, j, up] + uu[2, j, up]) - (
                    uu[0, j, down] + uu[1, j, down] + uu[2, j, down]
                )
                eta[j, here] = (
                    eta[j, here] - push * (total + (c[j + 2] - c[j])) + rt[level, j, here]
                )

        over_rows(depth, rows_of, *part)

    def begin(level, part=None):
        rim = 7 * (LEVELS - 1 - level)
        at = 7 * level + 1
        predict(rim + 6, part, at)
        source(rim + 5, level, part, at + 1)
        if level > 0:
            sweep(rim + 5, pa, pb, part, at + 1)
        sweep(rim + 4, pb, pa, part, at + 2)
        sweep(rim + 3, pa, pb, part, at + 3)
        sweep(rim + 2, pb, pa, part, at + 4)

    def step(level, part=None):
        rim = 7 * (LEVELS - 1 - level)
        at = 7 * level + 1
        begin(level, part)
        correct(rim + 1, level, part, at + 5)
        raise_surface(rim, level, part, at + 6)

    step(0, "inner")
    start(hm_copies)
    step(1, "inner")
    to_neighbours(g, ngx, x_copies[1:], "recv")

    def clear_columns(rows):
        nothing = jnp.zeros((JS, RIM, LANES), jnp.float32)
        eta[:, rows] = nothing
        for k in range(3):
            uu[k, :, rows] = nothing
            vv[k, :, rows] = nothing
        for level in range(LEVELS):
            rt[level, :, rows] = nothing

    @pl.when(g == 0)
    def _():
        clear_columns(before)

    @pl.when(g == ngx - 1)
    def _():
        clear_columns(after)
    for level in range(2):
        step(level, "outer")

    step(2)

    finish_recv(hm_copies)
    lane64 = lane_of((block, LANES)) < 64
    for part in range(nsec):
        for p in range(ngx // 2):
            one, two = rx[2 * p, part], rx[2 * p + 1, part]
            columns = pl.ds(p * LANES, LANES)
            hh[0, part, :, columns] = jnp.where(lane64, one, turn(two, 64))
            hh[1, part, :, columns] = jnp.where(lane64, turn(one, 64), two)
    band_columns = pl.ds(pl.multiple_of(b * tile_y, LANES), tile_y)
    h2_copies = []
    for which, out in enumerate((thick_out, mom_out)):
        for j in range(1, bands):
            device = along_band(j)
            h2_copies.append(
                remote(
                    hh.at[which, device[0], pl.ds(pl.multiple_of(device[2] * rc, 8), rc)],
                    out.at[:, band_columns],
                    h2_send.at[which, j], h2_recv.at[which, j], device,
                )
            )
    for which, out in enumerate((thick_out, mom_out)):
        h2_copies.append(
            pltpu.make_async_copy(
                hh.at[which, s, pl.ds(pl.multiple_of(y * rc, 8), rc)],
                out.at[:, band_columns],
                own_sem.at[6 + which],
            )
        )
    start(h2_copies)

    def turn_back(n, ref):
        for j in range(JS):
            back[n, pl.ds(j, LANES, stride=JS)] = ref[j, own_x].T

    begin(LEVELS - 1)
    for j in range(JS):
        back[4, pl.ds(j, LANES, stride=JS)] = (
            qq[j, own_x] + pa[2, j, own_x] * (1.0 / LEVELS)
        ).T
    b_copies = []
    columns = pl.ds(pl.multiple_of(g * LANES, LANES), LANES)
    for j in range(1, ngx):
        device = along_gx(j)
        b_copies.append(
            remote(
                back.at[4, strip_rows(device[1])], bottom_out.at[0, 0, :, columns],
                b_send.at[j], b_recv.at[j], device,
            )
        )
    b_copies.append(
        pltpu.make_async_copy(
            back.at[4, strip_rows(g)], bottom_out.at[0, 0, :, columns], own_sem.at[8]
        )
    )
    start(b_copies)
    correct(1, LEVELS - 1)
    for k in range(3):
        turn_back(1 + k, pa.at[k])
    outs = [
        pltpu.make_async_copy(back.at[pl.ds(1, 3), own_rows], press_out, out_sem.at[1]),
        pltpu.make_async_copy(back.at[0, own_rows], surf_out, out_sem.at[0]),
    ]
    outs[0].start()
    raise_surface(0, LEVELS - 1)
    turn_back(0, eta)
    outs[1].start()
    finish_recv(b_copies)
    for copy in h2_copies[:-2]:
        copy.wait_recv()
    for copy in h2_copies[-2:] + outs:
        copy.wait()
    for copies in rises + [hm_copies, b_copies]:
        for copy in copies[:-1]:
            copy.wait_send()
    to_neighbours(b, bands, relay + y_copies, "sent")
    to_neighbours(g, ngx, x_copies, "sent")
    for copy in h2_copies[:-2]:
        copy.wait_send()


def write_results(*refs):
    count = (len(refs) - 2) // 3
    given, results, held = refs[:count], refs[count : 2 * count], refs[2 * count : 3 * count]
    in_sem, out_sem = refs[3 * count :]
    ins = [pltpu.make_async_copy(given[n], held[n], in_sem.at[n]) for n in range(count)]
    outs = [pltpu.make_async_copy(held[n], results[n], out_sem.at[n]) for n in range(count)]
    for copy in ins:
        copy.start()
    for n in range(count):
        ins[n].wait()
        outs[n].start()
    for copy in outs:
        copy.wait()


def shards(
    slide_thickness, footprint, slide_momentum, bed_friction, surface, flux_x, flux_y,
    bathy_class, depth_table,
):
    nsec, ngx, ngy = (lax.axis_size(a) for a in ("sec", "gx", "gy"))
    _, _, strip_w, cells_x = slide_thickness.shape
    tile_y, tile_x = surface.shape
    assert tile_x == LANES and strip_w * 2 == LANES and strip_w * ngx == tile_y
    rc = cells_x // (nsec * ngx * ngy)
    bands = nsec * ngy
    x_rows = tile_x + 2 * TOP + 48
    f32 = jnp.float32
    one = (JS, x_rows, LANES)
    three = (3,) + one
    wide_rows = JS * LANES
    results = (
        jax.ShapeDtypeStruct(surface.shape, f32),
        jax.ShapeDtypeStruct(flux_x.shape, f32),
        jax.ShapeDtypeStruct(slide_thickness.shape, f32),
        jax.ShapeDtypeStruct((rc, tile_y * bands), f32),
        jax.ShapeDtypeStruct((rc, tile_y * bands), f32),
    )
    dma = pltpu.SemaphoreType.DMA
    anywhere = pl.BlockSpec(memory_space=pl.ANY)
    made = pl.pallas_call(
        functools.partial(kernel, (nsec, ngx, ngy, tile_y, strip_w, cells_x, rc)),
        out_shape=results,
        in_specs=[anywhere] * 8 + [pl.BlockSpec(memory_space=pltpu.SMEM)],
        out_specs=(anywhere,) * 5,
        scratch_shapes=[
            pltpu.VMEM((3, strip_w, cells_x), f32),
            pltpu.VMEM((strip_w, cells_x), jnp.int32),
            pltpu.VMEM((LEVELS, ngx, strip_w, LANES), f32),
            pltpu.VMEM((ngx, strip_w, LANES), f32),
            pltpu.VMEM((2 * strip_w, cells_x), f32),
            pltpu.VMEM((nsec, ngx, ngy * rc, LANES), f32),
            pltpu.VMEM((ngx, nsec, ngy * rc, LANES), f32),
            pltpu.VMEM((2, nsec, ngy * rc, tile_y), f32),
            pltpu.VMEM((8, wide_rows, LANES), f32),
            pltpu.VMEM((tile_y + 2 * RIM, LANES), jnp.int32),
            pltpu.VMEM((LEVELS + 1, wide_rows, LANES), f32),
            pltpu.VMEM((2, JS, RIM, LANES), f32),
            pltpu.VMEM((2, JS, RIM, LANES), f32),
            pltpu.VMEM((2, 3, JS, RIM, LANES), f32),
            pltpu.VMEM((2, 3, JS, RIM, LANES), f32),
            pltpu.VMEM(one, f32),
            pltpu.VMEM(three, f32),
            pltpu.VMEM(three, f32),
            pltpu.VMEM(one, f32),
            pltpu.VMEM(three, f32),
            pltpu.VMEM(three, f32),
            pltpu.VMEM(three, f32),
            pltpu.VMEM((5,) + one, f32),
            pltpu.VMEM(one, f32),
            pltpu.VMEM(one, f32),
            pltpu.VMEM((LEVELS,) + one, f32),
            pltpu.VMEM((5, wide_rows, LANES), f32),
            dma((8,)),
            dma((2,)),
            dma((2, 4)), dma((2, 4)),
            dma((LEVELS + 1, ngx)), dma((LEVELS + 1, ngx)),
            dma((2, LEVELS + 1)), dma((2, LEVELS + 1)),
            dma((2, 4)), dma((2, 4)),
            dma((ngx,)), dma((ngx,)),
            dma((2, bands)), dma((2, bands)),
            dma((ngx,)), dma((ngx,)),
            dma((9,)),
        ],
        compiler_params=pltpu.CompilerParams(
            collective_id=0, has_side_effects=True, vmem_limit_bytes=56 * 2**20
        ),
    )(
        slide_thickness, footprint, slide_momentum, bed_friction, surface, flux_x, flux_y,
        bathy_class, depth_table,
    )
    return pl.pallas_call(
        write_results,
        out_shape=results,
        in_specs=[anywhere] * 5,
        out_specs=(anywhere,) * 5,
        scratch_shapes=[pltpu.VMEM(r.shape, f32) for r in results] + [dma((5,)), dma((5,))],
    )(*made)


def solution(mesh):
    strips = P(("sec", "gy"), "gx", None, None)
    tiles = P(("sec", "gy"), "gx")
    layers = P(None, ("sec", "gy"), "gx")
    turned = P(("sec", "gx", "gy"), None)
    return jax.shard_map(
        shards,
        mesh=mesh,
        in_specs=(strips,) * 4 + (tiles, layers, layers, tiles, P()),
        out_specs=(tiles, layers, strips, turned, turned),
        check_vma=False,
    )
```
